256 devices in a mesh: group: 8 (over x, core), fsdp: 32 (over z, y).
Axes of the slice: x: 4, y: 4, z: 8, core: 2. Of those that a mesh axis runs over, the one named last changes fastest.
Arguments:
- hidden: bfloat16 [64, 128, 8192], P('group', None, 'fsdp'), may hold values from -6 to 6
- norm_gain: bfloat16 [8192], replicated, may hold values from 0.099609375 to 1.8984375
- w_query: bfloat16 [8192, 8192], P('group', 'fsdp'), may hold values from -0.0625 to 0.0625
- key_projection_weight: bfloat16 [8192, 1024], P('group'), may hold values from -0.0625 to 0.0625
- value_projection_weight: bfloat16 [8192, 1024], P('group'), may hold values from -0.0625 to 0.0625
- prompt_key_cache: bfloat16 [2048, 1024], P('group'), may hold values from -74 to 74
- prompt_value_cache: bfloat16 [2048, 1024], P('group'), may hold values from -6 to 6
- keep_flag: int32 [64], replicated, may hold values from 0 to 1, as said below
- destination: int32 [64], replicated, may hold values from 0 to 31, as said below
- row_counts: int32 [64], replicated, may hold values from 32 to 128
Outputs:
- attended: bfloat16 [32, 128, 8192], P('group', None, 'fsdp')
The draws below stay inside these ranges and needn't reach their ends.
Inputs may be any that keep to these rules, and one draw needn't show every extreme that they name: `keep_flag`: exactly 32 blocks are kept. `destination`: the kept blocks name the slots 0 to 31, each exactly once. Among the 8 blocks g * 8 to g * 8 + 7, the kept ones that name a slot of d * 4 to d * 4 + 3 number either 0 or exactly 1. Entries of dropped blocks are arbitrary slot numbers.
All inputs are finite; a program needn't handle non-finite values.
Results may differ from the reference program's by a relative error of at most 0.012.
The reference program's roundings to bfloat16 on the way count: a program that leaves them out, or rounds other values in their place, can miss the bound.
Values may be sent and summed in bfloat16 or wider, within the bound.
No kernel may reach another device: no remote copies, remote signals or barrier semaphores. Data moves between devices by JAX's collectives and lax.ppermute only.
A program may use at most 128 MiB of HBM per device.

```python
import jax
import jax.numpy as jnp
from jax import lax

MODEL_WIDTH = 8192
QUERY_HEADS = 64
KEY_VALUE_HEADS = 8
HEAD_SIZE = 128
BLOCK_TOKENS = 128
PROMPT_TOKENS = 2048
IN_DEV = 8
CAP = 1
OUT_DEV = 4
BLOCKS = 64
SLOTS = 32


def route_plan(key):
    group_total = BLOCKS // IN_DEV
    pick_keys = jax.random.split(key, 4)
    pool_copies = min(IN_DEV // CAP, group_total)
    pick_pool = jnp.tile(jnp.arange(group_total, dtype=jnp.int32), pool_copies)
    pick_pool = jax.random.permutation(pick_keys[0], pick_pool)
    chosen = jnp.sort(pick_pool[:group_total * (OUT_DEV // CAP)])
    pick_index = jnp.arange(chosen.shape[0], dtype=jnp.int32)
    dest_order = jax.random.permutation(pick_keys[1], group_total).astype(jnp.int32)
    target_dev = dest_order[pick_index % group_total]
    slot_base = pick_index // group_total * CAP
    earlier = (chosen[None, :] == chosen[:, None]) & (pick_index[None, :] < pick_index[:, None])
    pick_rank = jnp.sum(earlier.astype(jnp.int32), axis=1)
    slot_perm = jax.vmap(lambda sub_key: jax.random.permutation(sub_key, IN_DEV))(jax.random.split(pick_keys[2], group_total)).astype(jnp.int32)
    keep_flags = jnp.zeros((BLOCKS,), jnp.int32)
    dest_slots = jax.random.randint(pick_keys[3], (BLOCKS,), 0, OUT_DEV * group_total, dtype=jnp.int32)
    for copy_index in range(CAP):
        block_ids = chosen * IN_DEV + slot_perm[chosen, pick_rank * CAP + copy_index]
        keep_flags = keep_flags.at[block_ids].set(1)
        dest_slots = dest_slots.at[block_ids].set(target_dev * OUT_DEV + slot_base + copy_index)
    return (keep_flags, dest_slots)


def draw_keep_flag(key, part):
    return route_plan(key)[0]


def draw_destination(key, part):
    return route_plan(key)[1]


def draw_prompt_key_cache(key, part):
    key = jax.random.fold_in(key, 7)
    jitter_random_key, position_random_key, polarity_random_key, permute_random_key = jax.random.split(key, 4)
    random_jitter = jnp.clip(jax.random.normal(jitter_random_key, (PROMPT_TOKENS, KEY_VALUE_HEADS, HEAD_SIZE), jnp.float32), -6.0, 6.0)
    lower_limit = 30.0
    upper_limit = 64.0
    head_permuted_order = jax.random.permutation(permute_random_key, KEY_VALUE_HEADS).astype(jnp.float32)
    jitter_scale = lower_limit * (upper_limit / lower_limit) ** (head_permuted_order / (KEY_VALUE_HEADS - 1))
    token_positions = jax.random.permutation(position_random_key, PROMPT_TOKENS)[:2 * KEY_VALUE_HEADS].astype(jnp.int32).reshape(KEY_VALUE_HEADS, 2)
    rows = jnp.arange(PROMPT_TOKENS, dtype=jnp.int32)
    planted = jnp.any(rows[:, None, None] == token_positions[None, :, :], axis=2).astype(jnp.float32)
    sign_flips = (2 * jax.random.randint(polarity_random_key, (KEY_VALUE_HEADS, HEAD_SIZE), 0, 2) - 1).astype(jnp.float32)
    joined_keys = random_jitter + planted[:, :, None] * jitter_scale[None, :, None] * sign_flips[None, :, :]
    return joined_keys.reshape(PROMPT_TOKENS, KEY_VALUE_HEADS * HEAD_SIZE).astype(jnp.bfloat16)


def touch_ends(entries, stream_key, smallest, largest):
    longest = entries.shape.index(max(entries.shape))
    spots = []
    for shift in (0, 1):
        where = [jax.random.randint(jax.random.fold_in(stream_key, axis), (), 0, length) for axis, length in enumerate(entries.shape)]
        where[longest] = (where[longest] + shift) % entries.shape[longest]
        spots.append(tuple(where))
    return entries.at[spots[0]].set(smallest).at[spots[1]].set(largest)


def block_levels(key, dims, cuts, least, high):
    loudness, own = 1.0, jax.random.fold_in(key, 6)
    for dim, parts in cuts:
        heights = jnp.exp(jax.random.uniform(jax.random.fold_in(own, dim), (parts,), jnp.float32, least / len(cuts), high / len(cuts)))
        loudness = loudness * jnp.repeat(heights, dims[dim] // parts).reshape([-1 if axis == dim else 1 for axis in range(len(dims))])
    return loudness


def noise(rng, dims, spread, reach, cuts=(), held_as=jnp.bfloat16):
    drawn = jax.random.normal(rng, dims, jnp.float32) * spread
    if len(cuts) > 0:
        drawn = block_levels(rng, dims, cuts, -0.22, 0.18) * drawn
    return jnp.clip(drawn, min=-reach, max=reach).astype(held_as)


def setup_inputs(seed: int = 0) -> dict:
    keys = jax.random.split(jax.random.key(seed), 11)
    return {
        "hidden": noise(keys[0], (BLOCKS, BLOCK_TOKENS, MODEL_WIDTH), 1.0, 6.0, ((0, 8), (2, 32))),
        "norm_gain": jnp.clip(1.0 + 0.18 * jax.random.normal(keys[1], (MODEL_WIDTH,), jnp.float32), 0.099609375, 1.8984375).astype(jnp.bfloat16),
        "w_query": noise(keys[2], (MODEL_WIDTH, QUERY_HEADS * HEAD_SIZE), MODEL_WIDTH ** -0.5, 0.0625, ((0, 8), (1, 32))),
        "key_projection_weight": noise(keys[3], (MODEL_WIDTH, KEY_VALUE_HEADS * HEAD_SIZE), MODEL_WIDTH ** -0.5, 0.0625, ((0, 8),)),
        "value_projection_weight": noise(keys[4], (MODEL_WIDTH, KEY_VALUE_HEADS * HEAD_SIZE), MODEL_WIDTH ** -0.5, 0.0625, ((0, 8),)),
        "prompt_key_cache": draw_prompt_key_cache(jax.random.fold_in(keys[10], 71), 0),
        "prompt_value_cache": noise(keys[6], (PROMPT_TOKENS, KEY_VALUE_HEADS * HEAD_SIZE), 1.0, 6.0, ((0, 8),)),
        "keep_flag": draw_keep_flag(jax.random.fold_in(keys[10], 71), 0),
        "destination": draw_destination(jax.random.fold_in(keys[10], 71), 0),
        "row_counts": touch_ends(jax.random.randint(keys[9], (BLOCKS,), BLOCK_TOKENS // 4, BLOCK_TOKENS + 1), jax.random.fold_in(keys[9], 1), BLOCK_TOKENS // 4, BLOCK_TOKENS).astype(jnp.int32),
    }


EPSILON = 1e-05
ROPE_THETA = 500000.0
CONTEXT_BASE = 8192.0
STRETCH = 8.0
MASKED_SCORE = -1e+30

def rope_tables(length, offset):
    half_dim = HEAD_SIZE // 2
    base_rate = ROPE_THETA ** (-(jnp.arange(half_dim, dtype=jnp.float32) * 2.0 / HEAD_SIZE))
    ratio = CONTEXT_BASE * base_rate / (2.0 * jnp.pi)
    smooth = jnp.clip((ratio - 1.0) / 3.0, 0.0, 1.0)
    inverse_rate = (1.0 - smooth) * base_rate / STRETCH + smooth * base_rate
    token_positions = jnp.arange(length, dtype=jnp.float32) + offset
    angles = token_positions[:, None] * inverse_rate[None, :]
    return (jnp.cos(angles), jnp.sin(angles))

def rotate(values, cosine, sine_table):
    half_dim = values.shape[-1] // 2
    first_half = values[..., :half_dim]
    second = values[..., half_dim:]
    cosine = cosine[:, None, :]
    sine_table = sine_table[:, None, :]
    return jnp.concatenate([first_half * cosine - second * sine_table, second * cosine + first_half * sine_table], axis=-1)

def reference(hidden, norm_gain, w_query, key_projection_weight, value_projection_weight, prompt_key_cache, prompt_value_cache, keep_flag, destination, row_counts):
    block_total = keep_flag.shape[0]
    slot_ids = jnp.arange(SLOTS, dtype=jnp.int32)
    matched = (keep_flag[None, :] == 1) & (destination[None, :] == slot_ids[:, None])
    sources = lax.optimization_barrier(jnp.sum(jnp.where(matched, jnp.arange(block_total, dtype=jnp.int32)[None, :], 0), axis=1)).astype(jnp.int32)
    cosine, sine_table = rope_tables(BLOCK_TOKENS, PROMPT_TOKENS)
    query_group_width = QUERY_HEADS // KEY_VALUE_HEADS
    score_scale = HEAD_SIZE ** (-0.5)
    prompt_keys = prompt_key_cache.reshape(PROMPT_TOKENS, KEY_VALUE_HEADS, HEAD_SIZE)
    prompt_values = prompt_value_cache.reshape(PROMPT_TOKENS, KEY_VALUE_HEADS, HEAD_SIZE)
    position = jnp.arange(BLOCK_TOKENS, dtype=jnp.int32)
    columns = jnp.arange(PROMPT_TOKENS + BLOCK_TOKENS, dtype=jnp.int32)
    gain_wide = norm_gain.astype(jnp.float32)

    def one_block(source_block):
        block_rows = hidden[source_block].astype(jnp.float32)
        valid_rows = row_counts[source_block]
        normalized_input = (block_rows * lax.rsqrt(lax.optimization_barrier(jnp.mean(block_rows * block_rows, axis=1, keepdims=True)) + EPSILON) * gain_wide).astype(jnp.bfloat16)
        query_vectors = jnp.dot(normalized_input, w_query, preferred_element_type=jnp.float32).reshape(BLOCK_TOKENS, QUERY_HEADS, HEAD_SIZE)
        fresh_keys = jnp.dot(normalized_input, key_projection_weight, preferred_element_type=jnp.float32).reshape(BLOCK_TOKENS, KEY_VALUE_HEADS, HEAD_SIZE)
        fresh_values = jnp.dot(normalized_input, value_projection_weight, preferred_element_type=jnp.float32).reshape(BLOCK_TOKENS, KEY_VALUE_HEADS, HEAD_SIZE)
        query_vectors = rotate(query_vectors, cosine, sine_table).astype(jnp.bfloat16)
        fresh_keys = rotate(fresh_keys, cosine, sine_table).astype(jnp.bfloat16)
        fresh_values = fresh_values.astype(jnp.bfloat16)
        all_keys = jnp.concatenate([prompt_keys, fresh_keys], axis=0).astype(jnp.float32)
        all_values = jnp.concatenate([prompt_values, fresh_values], axis=0).astype(jnp.float32)
        grouped_queries = query_vectors.reshape(BLOCK_TOKENS, KEY_VALUE_HEADS, query_group_width, HEAD_SIZE).astype(jnp.float32)
        scores = jnp.einsum('qhgd,khd->qhgk', grouped_queries, all_keys) * score_scale
        own_column = columns[None, :] - PROMPT_TOKENS
        allowed = (columns[None, :] < PROMPT_TOKENS) | (own_column <= position[:, None]) & (own_column < valid_rows)
        scores = jnp.where(allowed[:, None, None, :], scores, MASKED_SCORE)
        row_max = lax.optimization_barrier(jnp.max(scores, axis=3, keepdims=True))
        powers = jnp.exp(scores - row_max)
        row_sum = lax.optimization_barrier(jnp.sum(powers, axis=3))
        weights = lax.optimization_barrier(powers.astype(jnp.bfloat16)).astype(jnp.float32)
        mixed_out = jnp.einsum('qhgk,khd->qhgd', weights, all_values) / row_sum[..., None]
        live_rows = (position < valid_rows)[:, None, None, None]
        return jnp.where(live_rows, mixed_out, 0.0).reshape(BLOCK_TOKENS, QUERY_HEADS * HEAD_SIZE).astype(jnp.bfloat16)
    return lax.map(one_block, sources)
```

```python
import functools

import jax
import jax.numpy as jnp
from jax import lax
from jax.experimental import pallas as pl
from jax.experimental.pallas import tpu as pltpu
from jax.sharding import PartitionSpec as P

HEAD_SIZE = 128
PROMPT_TOKENS = 2048
IN_DEV = 8
OUT_DEV = 4
ROWS = 128
XS, CORES, ZS, YS = 4, 2, 8, 4
TILE = 256
MODEL_WIDTH = 8192

EPSILON = 1e-05
ROPE_THETA = 500000.0
CONTEXT_BASE = 8192.0
STRETCH = 8.0
MASKED_SCORE = -1e30

RELS = [(dx, dc) for dx in range(XS) for dc in range(CORES)]


def group_perm(dx, dc):
    return [
        (x * CORES + c, ((x + dx) % XS) * CORES + (c ^ dc)) for x in range(XS) for c in range(CORES)
    ]


def z_perm(d):
    return [(z * YS + y, ((z + d) % ZS) * YS + y) for z in range(ZS) for y in range(YS)]


def y_perm(d):
    return [(z * YS + y, z * YS + (y + d) % YS) for z in range(ZS) for y in range(YS)]


def send_group(v, dx, dc):
    return lax.ppermute(v, "group", group_perm(dx, dc))


def send_z(v, d):
    return lax.ppermute(v, "fsdp", z_perm(d))


def send_y(v, d):
    return lax.ppermute(v, "fsdp", y_perm(d))


def rope_tables(length, offset):
    half_dim = HEAD_SIZE // 2
    base_rate = ROPE_THETA ** (-(jnp.arange(half_dim, dtype=jnp.float32) * 2.0 / HEAD_SIZE))
    ratio = CONTEXT_BASE * base_rate / (2.0 * jnp.pi)
    smooth = jnp.clip((ratio - 1.0) / 3.0, 0.0, 1.0)
    inverse_rate = (1.0 - smooth) * base_rate / STRETCH + smooth * base_rate
    token_positions = jnp.arange(length, dtype=jnp.float32) + offset
    angles = token_positions[:, None] * inverse_rate[None, :]
    cosine, sine = jnp.cos(angles), jnp.sin(angles)
    return (
        jnp.concatenate([cosine, cosine], axis=1),
        jnp.concatenate([-sine, sine], axis=1),
    )


def swap_halves(v):
    half = HEAD_SIZE // 2
    return jnp.concatenate([v[:, half:], v[:, :half]], axis=1)


ANY = pl.BlockSpec(memory_space=pl.ANY)
VMEM = pl.BlockSpec(memory_space=pltpu.VMEM)
SMEM = pl.BlockSpec(memory_space=pltpu.SMEM)


def shaped(shape, dtype):
    return jax.ShapeDtypeStruct(shape, dtype)


def pack_kernel(meta, hidden, wq, wk, wv, kc, vc, *rest):
    outs, sems = rest[:-1], rest[-1]
    blocks, own, parts = outs[:8], outs[8], outs[9:12]
    z = meta[8]
    y = meta[9]
    cols = pl.ds(pl.multiple_of(z * HEAD_SIZE, HEAD_SIZE), HEAD_SIZE)
    rows = pl.ds(pl.multiple_of(y * TILE, TILE), TILE)
    copies = [(hidden.at[meta[i]], blocks[i]) for i in range(8)]
    for r in range(1, 4):
        other = lax.rem(y + YS - r, YS)
        copies.append(
            (wq.at[pl.ds(pl.multiple_of(other * TILE, TILE), TILE)], parts[r - 1])
        )
    copies.append((wq.at[rows], own.at[0]))
    copies.append((wk.at[rows, cols], own.at[1, :, pl.ds(0, HEAD_SIZE)]))
    copies.append((wv.at[rows, cols], own.at[1, :, pl.ds(HEAD_SIZE, HEAD_SIZE)]))
    copies.append((kc.at[:, cols], own.at[2, :, pl.ds(0, HEAD_SIZE)]))
    copies.append((vc.at[:, cols], own.at[2, :, pl.ds(HEAD_SIZE, HEAD_SIZE)]))
    started = [pltpu.make_async_copy(s, d, sems.at[i]) for i, (s, d) in enumerate(copies)]
    for copy in started:
        copy.start()
    for copy in started:
        copy.wait()


def pack(meta, hidden, wq, wk, wv, kc, vc):
    bf16 = jnp.bfloat16
    out_shape = (
        [shaped((ROWS, TILE), bf16)] * 8
        + [shaped((3, TILE, TILE), bf16)]
        + [shaped((TILE, TILE), bf16)] * 3
    )
    return pl.pallas_call(
        pack_kernel,
        out_shape=out_shape,
        in_specs=[SMEM] + [ANY] * 6,
        out_specs=[ANY] * 12,
        scratch_shapes=[pltpu.SemaphoreType.DMA((16,))],
        name="pack",
    )(meta, hidden, wq, wk, wv, kc, vc)


def unpack_kernel(source, *refs):
    pieces, x_ref, ss_ref = refs[:8], refs[8], refs[9]
    ones = jnp.ones((8, TILE), jnp.float32)
    for j in range(OUT_DEV):
        rows = pl.ds(j * ROWS, ROWS)
        for i in range(8):

            @pl.when(source[j] == i)
            def _():
                x_ref[rows, :] = pieces[i][...]

        wide = x_ref[rows, :].astype(jnp.float32)
        sums = lax.dot_general(
            ones,
            wide * wide,
            (((1,), (1,)), ((), ())),
            precision=lax.Precision.HIGHEST,
            preferred_element_type=jnp.float32,
        )
        ss_ref[pl.ds(j, 1), :] = sums[0:1, :]


def unpack(source, pieces):
    return pl.pallas_call(
        unpack_kernel,
        out_shape=[
            shaped((OUT_DEV * ROWS, TILE), jnp.bfloat16),
            shaped((OUT_DEV, ROWS), jnp.float32),
        ],
        in_specs=[SMEM] + [VMEM] * 8,
        out_specs=[VMEM] * 2,
        name="unpack",
    )(source, *pieces)


SHARDS = 8


def project_kernel(meta, scale, gain, *refs):
    shards, weights = refs[:9], refs[9:19]
    own_ref, kv_ref, o1, o2, o3 = refs[19:24]
    normed, wide_w, sems = refs[24:]
    copies = []

    def bring(src, first, last, position):
        base = pl.ds(pl.multiple_of(meta[8 + position] * TILE, TILE), TILE)
        for n in range(first, last):
            copies.append(
                pltpu.make_async_copy(
                    src.at[n - first], wide_w.at[n, base], sems.at[len(copies)]
                )
            )
            copies[-1].start()

    for half in range(2):
        own, left, right, far_a, far_b = weights[5 * half : 5 * half + 5]
        bring(own, 0, 5, 4 * half)
        bring(left, 0, 5, 4 * half + 1)
        bring(right, 0, 5, 4 * half + 2)
        bring(far_a, 0, 3, 4 * half + 3)
        bring(far_b, 3, 5, 4 * half + 3)

    def norm(src, rows, position):
        k = meta[position]
        cols = pl.ds(pl.multiple_of(k * TILE, TILE), TILE)
        normed[rows, cols] = (
            src[...].astype(jnp.float32) * scale[rows, :] * gain[pl.ds(k, 1), :]
        ).astype(jnp.bfloat16)

    every = pl.ds(0, OUT_DEV * ROWS)
    for s in range(7):
        norm(shards[s], every, s)
    half_rows = OUT_DEV * ROWS // 2
    norm(shards[7], pl.ds(0, half_rows), 7)
    norm(shards[8], pl.ds(half_rows, half_rows), 7)
    for copy in copies:
        copy.wait()

    def product(n):
        return jnp.dot(normed[...], wide_w[n], preferred_element_type=jnp.float32)

    kv_ref[...] = product(4)
    for n, out in ((1, o1), (2, o2), (3, o3)):
        out[...] = product(n).astype(jnp.bfloat16)
    own_ref[...] = product(0)


def project(meta, scale, gain, shards, weights):
    total = OUT_DEV * ROWS
    return pl.pallas_call(
        project_kernel,
        out_shape=[shaped((total, TILE), jnp.float32)] * 2
        + [shaped((total, TILE), jnp.bfloat16)] * 3,
        in_specs=[SMEM] + [VMEM] * 2 + [VMEM] * 9 + [ANY] * 10,
        out_specs=[VMEM] * 5,
        scratch_shapes=[
            pltpu.VMEM((total, SHARDS * TILE), jnp.bfloat16),
            pltpu.VMEM((5, SHARDS * TILE, TILE), jnp.bfloat16),
            pltpu.SemaphoreType.DMA((40,)),
        ],
        compiler_params=pltpu.CompilerParams(vmem_limit_bytes=40 * 2**20),
        cost_estimate=pl.CostEstimate(
            flops=2 * total * 2048 * 1280, bytes_accessed=10 * 2**20, transcendentals=0
        ),
        name="project",
    )(meta, scale, gain, *shards, *weights)


def attend_kernel(meta, own, o1, o2, o3, cosine, sine, fresh, *refs):
    caches, out_ref, keys, values = refs[:8], refs[8], refs[9], refs[10]
    slot = pl.program_id(0)
    part = TILE

    @pl.when(slot == 0)
    def _():
        for i, cache in enumerate(caches):
            keys[pl.ds(i * part, part), :] = cache[0, :, :HEAD_SIZE]
            values[pl.ds(i * part, part), :] = cache[0, :, HEAD_SIZE:]

    keys[pl.ds(PROMPT_TOKENS, ROWS), :] = fresh[0, :, :HEAD_SIZE]
    values[pl.ds(PROMPT_TOKENS, ROWS), :] = fresh[0, :, HEAD_SIZE:]
    q = own[...] + o1[...].astype(jnp.float32) + o2[...].astype(jnp.float32)
    q = q + o3[...].astype(jnp.float32)
    turned = []
    for h in range(2):
        v = q[:, h * HEAD_SIZE : (h + 1) * HEAD_SIZE]
        turned.append((v * cosine[...] + swap_halves(v) * sine[...]).astype(jnp.bfloat16))
    queries = jnp.concatenate(turned, axis=0)
    scores = lax.dot_general(
        queries, keys[...], (((1,), (1,)), ((), ())), preferred_element_type=jnp.float32
    ) * (HEAD_SIZE**-0.5)
    valid = meta[slot]
    row = lax.broadcasted_iota(jnp.int32, (2 * ROWS, ROWS), 0) % ROWS
    column = lax.broadcasted_iota(jnp.int32, (2 * ROWS, ROWS), 1)
    allowed = (column <= row) & (column < valid)
    old = scores[:, :PROMPT_TOKENS]
    new = jnp.where(allowed, scores[:, PROMPT_TOKENS:], MASKED_SCORE)
    top = jnp.maximum(
        jnp.max(old, axis=1, keepdims=True), jnp.max(new, axis=1, keepdims=True)
    )
    old, new = jnp.exp(old - top), jnp.exp(new - top)
    total = jnp.sum(old, axis=1, keepdims=True) + jnp.sum(new, axis=1, keepdims=True)
    mixed = jnp.dot(
        old.astype(jnp.bfloat16), values[:PROMPT_TOKENS, :], preferred_element_type=jnp.float32
    ) + jnp.dot(
        new.astype(jnp.bfloat16), values[PROMPT_TOKENS:, :], preferred_element_type=jnp.float32
    )
    mixed = jnp.where(row < valid, mixed / total, 0.0).astype(jnp.bfloat16)
    out_ref[0, :, :HEAD_SIZE] = mixed[:ROWS]
    out_ref[0, :, HEAD_SIZE:] = mixed[ROWS:]


def attend(meta, own, others, cosine, sine, fresh, caches, cache_blocks):
    by_slot = pl.BlockSpec((ROWS, TILE), lambda j, m: (j, 0))
    table = pl.BlockSpec((ROWS, HEAD_SIZE), lambda j, m: (0, 0))

    def cache_spec(block):
        return pl.BlockSpec((1, TILE, TILE), lambda j, m: (block, 0, 0))

    return pl.pallas_call(
        attend_kernel,
        out_shape=shaped((OUT_DEV, ROWS, TILE), jnp.bfloat16),
        grid_spec=pltpu.PrefetchScalarGridSpec(
            num_scalar_prefetch=1,
            grid=(OUT_DEV,),
            in_specs=[by_slot] * 4
            + [table] * 2
            + [pl.BlockSpec((1, ROWS, TILE), lambda j, m: (m[4 + j], 0, 0))]
            + [cache_spec(b) for b in cache_blocks],
            out_specs=pl.BlockSpec((1, ROWS, TILE), lambda j, m: (j, 0, 0)),
            scratch_shapes=[
                pltpu.VMEM((PROMPT_TOKENS + ROWS, HEAD_SIZE), jnp.bfloat16),
                pltpu.VMEM((PROMPT_TOKENS + ROWS, HEAD_SIZE), jnp.bfloat16),
            ],
        ),
        compiler_params=pltpu.CompilerParams(vmem_limit_bytes=40 * 2**20),
        cost_estimate=pl.CostEstimate(
            flops=4 * 1024 * 2176 * 128, bytes_accessed=4 * 2**20, transcendentals=1024 * 2176
        ),
        name="attend",
    )(meta, own, *others, cosine, sine, fresh, *caches)


def body(
    hidden,
    norm_gain,
    w_query,
    key_projection_weight,
    value_projection_weight,
    prompt_key_cache,
    prompt_value_cache,
    keep_flag,
    destination,
    row_counts,
):
    g = lax.axis_index("group")
    f = lax.axis_index("fsdp")
    x, c = g // CORES, g % CORES
    z, y = f // YS, f % YS

    block_ids = jnp.arange(keep_flag.shape[0], dtype=jnp.int32)
    live = keep_flag == 1
    targets = jnp.stack([((x + dx) % XS) * CORES + (c ^ dc) for dx, dc in RELS])
    mine = live & (block_ids // IN_DEV == g)
    chosen = jnp.sum(
        jnp.where(
            mine[None, :] & (destination[None, :] // OUT_DEV == targets[:, None]),
            block_ids[None, :] % IN_DEV,
            0,
        ),
        axis=1,
    )
    slots = g * OUT_DEV + jnp.arange(OUT_DEV, dtype=jnp.int32)
    matched = live[None, :] & (destination[None, :] == slots[:, None])
    sources = jnp.sum(jnp.where(matched, block_ids[None, :], 0), axis=1)
    lengths = jnp.sum(jnp.where(matched, row_counts[None, :], 0), axis=1)
    source_group = sources // IN_DEV
    source_rel = ((x - source_group // CORES) % XS) * CORES + (c ^ (source_group % CORES))

    pack_meta = jnp.concatenate([chosen, jnp.stack([z, y])]).astype(jnp.int32)
    packed = pack(
        pack_meta,
        hidden,
        w_query,
        key_projection_weight,
        value_projection_weight,
        prompt_key_cache,
        prompt_value_cache,
    )
    blocks, own_parts, w_parts = packed[:8], packed[8], packed[9:12]

    pieces = [
        blocks[i] if rel == (0, 0) else send_group(blocks[i], *rel) for i, rel in enumerate(RELS)
    ]
    rows, squares = unpack(source_rel.astype(jnp.int32), pieces)

    for bit in (1, 2, 4, 8, 16):
        squares = squares + lax.ppermute(squares, "fsdp", [(i, i ^ bit) for i in range(ZS * YS)])
    scale = lax.rsqrt(squares / MODEL_WIDTH + EPSILON).reshape(OUT_DEV * ROWS, 1)

    fwd, bwd = [rows], [rows]
    for _ in range(3):
        fwd.append(send_z(fwd[-1], 1))
        bwd.append(send_z(bwd[-1], -1))
    half = OUT_DEV * ROWS // 2
    far = [send_z(fwd[3][:half], 1), send_z(bwd[3][half:], -1)]
    shards = fwd + bwd[1:] + far
    shard_ids = [(z - s) % ZS for s in range(4)] + [(z + s) % ZS for s in (1, 2, 3)] + [(z + 4) % ZS]

    arrived = [send_y(w_parts[r - 1], -r) for r in (1, 2, 3)]
    own = jnp.concatenate([own_parts[:1], jnp.stack(arrived), own_parts[1:]], axis=0)
    left, right = send_group(own, 1, 0), send_group(own, -1, 0)
    far_a, far_b = send_group(left[:3], 1, 0), send_group(right[3:], -1, 0)
    same_core = [own, left, right, far_a, far_b]
    other_core = [send_group(v, 0, 1) for v in same_core]
    weights = same_core + other_core
    weight_ids = [
        ((x + dx) % XS) * CORES + cc for cc in (c, 1 - c) for dx in (0, -1, 1, 2)
    ]

    gain = norm_gain.reshape(ZS, YS, TILE)
    gain = lax.dynamic_index_in_dim(gain, y, 1, keepdims=False).astype(jnp.float32)
    meta = jnp.stack(shard_ids + weight_ids).astype(jnp.int32)
    q_own, kv_own, *q_others = project(meta, scale, gain, shards, weights)

    kv_slots = kv_own.reshape(OUT_DEV, ROWS, TILE)
    kv = lax.dynamic_index_in_dim(kv_slots, y, 0, keepdims=False)
    for r in (1, 2, 3):
        part = lax.dynamic_index_in_dim(kv_slots, (y + r) % YS, 0, keepdims=False)
        kv = kv + send_y(part.astype(jnp.bfloat16), r).astype(jnp.float32)
    q_parts = [send_y(v, r) for r, v in zip((1, 2, 3), q_others)]

    cosine, sine = rope_tables(ROWS, PROMPT_TOKENS)
    key = kv[:, :HEAD_SIZE]
    key = (key * cosine + swap_halves(key) * sine).astype(jnp.bfloat16)
    fresh_own = jnp.concatenate([key, kv[:, HEAD_SIZE:].astype(jnp.bfloat16)], axis=1)
    fresh = jnp.stack([fresh_own] + [send_y(fresh_own, r) for r in (1, 2, 3)])
    fresh_ids = (y - jnp.arange(OUT_DEV, dtype=jnp.int32)) % YS

    caches, cache_blocks = [], []
    for part in (same_core, other_core):
        caches += [part[0], part[1], part[2], part[4]]
        cache_blocks += [5, 5, 5, 2]
    return attend(
        jnp.concatenate([lengths, fresh_ids]).astype(jnp.int32),
        q_own,
        q_parts,
        cosine,
        sine,
        fresh,
        caches,
        cache_blocks,
    )


def solution(mesh):
    return jax.shard_map(
        body,
        mesh=mesh,
        in_specs=(
            P("group", None, "fsdp"),
            P(),
            P("group", "fsdp"),
            P("group", None),
            P("group", None),
            P("group", None),
            P("group", None),
            P(),
            P(),
            P(),
        ),
        out_specs=P("group", None, "fsdp"),
        check_vma=False,
    )
```

```python
import functools

import jax
import jax.numpy as jnp
from jax import lax
from jax.experimental import pallas as pl
from jax.experimental.pallas import tpu as pltpu
from jax.sharding import PartitionSpec as P

HEAD_SIZE = 128
PROMPT_TOKENS = 2048
IN_DEV = 8
OUT_DEV = 4
ROWS = 128
XS, CORES, ZS, YS = 4, 2, 8, 4
TILE = 256
MODEL_WIDTH = 8192

EPSILON = 1e-05
ROPE_THETA = 500000.0
CONTEXT_BASE = 8192.0
STRETCH = 8.0
MASKED_SCORE = -1e30

def group_perm(dx, dc):
    return [
        (x * CORES + c, ((x + dx) % XS) * CORES + (c ^ dc)) for x in range(XS) for c in range(CORES)
    ]


def z_perm(d):
    return [(z * YS + y, ((z + d) % ZS) * YS + y) for z in range(ZS) for y in range(YS)]


def y_perm(d):
    return [(z * YS + y, z * YS + (y + d) % YS) for z in range(ZS) for y in range(YS)]


def send_group(v, dx, dc):
    return lax.ppermute(v, "group", group_perm(dx, dc))


def send_z(v, d):
    return lax.ppermute(v, "fsdp", z_perm(d))


def send_y(v, d):
    return lax.ppermute(v, "fsdp", y_perm(d))


def rope_tables(length, offset):
    half_dim = HEAD_SIZE // 2
    base_rate = ROPE_THETA ** (-(jnp.arange(half_dim, dtype=jnp.float32) * 2.0 / HEAD_SIZE))
    ratio = CONTEXT_BASE * base_rate / (2.0 * jnp.pi)
    smooth = jnp.clip((ratio - 1.0) / 3.0, 0.0, 1.0)
    inverse_rate = (1.0 - smooth) * base_rate / STRETCH + smooth * base_rate
    token_positions = jnp.arange(length, dtype=jnp.float32) + offset
    angles = token_positions[:, None] * inverse_rate[None, :]
    cosine, sine = jnp.cos(angles), jnp.sin(angles)
    return (
        jnp.concatenate([cosine, cosine], axis=1),
        jnp.concatenate([-sine, sine], axis=1),
    )


def swap_halves(v):
    half = HEAD_SIZE // 2
    return jnp.concatenate([v[:, half:], v[:, :half]], axis=1)


ANY = pl.BlockSpec(memory_space=pl.ANY)
VMEM = pl.BlockSpec(memory_space=pltpu.VMEM)
SMEM = pl.BlockSpec(memory_space=pltpu.SMEM)


def shaped(shape, dtype):
    return jax.ShapeDtypeStruct(shape, dtype)


def pack_kernel(place, keep, destination, hidden, wq, wk, wv, kc, vc, *rest):
    outs, parts, own, chosen, sems = rest[0:4], rest[4:7], rest[7], rest[8], rest[9]
    x, c, z, y = place[0], place[1], place[2], place[3]
    first = (x * CORES + c) * IN_DEV
    for i in range(8):
        chosen[i] = 0
    for b in range(IN_DEV):

        @pl.when(keep[first + b] == 1)
        def _():
            target = destination[first + b] // OUT_DEV
            dx = lax.rem(target // CORES + XS - x, XS)
            dc = lax.rem(target + c, CORES)
            chosen[dx * CORES + dc] = b

    cols = pl.ds(pl.multiple_of(z * HEAD_SIZE, HEAD_SIZE), HEAD_SIZE)
    rows = pl.ds(pl.multiple_of(y * TILE, TILE), TILE)
    copies = []
    for dx in range(XS):
        for dc in range(CORES):
            copies.append((hidden.at[chosen[dx * CORES + dc]], outs[dx].at[dc]))
    for r in range(1, 4):
        other = lax.rem(y + YS - r, YS)
        copies.append((wq.at[pl.ds(pl.multiple_of(other * TILE, TILE), TILE)], parts[r - 1]))
    copies.append((wq.at[rows], own.at[0]))
    copies.append((wk.at[rows, cols], own.at[1, :, pl.ds(0, HEAD_SIZE)]))
    copies.append((wv.at[rows, cols], own.at[1, :, pl.ds(HEAD_SIZE, HEAD_SIZE)]))
    copies.append((kc.at[:, cols], own.at[2, :, pl.ds(0, HEAD_SIZE)]))
    copies.append((vc.at[:, cols], own.at[2, :, pl.ds(HEAD_SIZE, HEAD_SIZE)]))
    started = [pltpu.make_async_copy(s, d, sems.at[i]) for i, (s, d) in enumerate(copies)]
    for copy in started:
        copy.start()
    for copy in started:
        copy.wait()


def pack(place, keep, destination, *arrays):
    bf16 = jnp.bfloat16
    return pl.pallas_call(
        pack_kernel,
        out_shape=[shaped((CORES, ROWS, TILE), bf16)] * 4
        + [shaped((TILE, TILE), bf16)] * 3
        + [shaped((3, TILE, TILE), bf16)],
        in_specs=[SMEM] * 3 + [ANY] * 6,
        out_specs=[VMEM] * 8,
        scratch_shapes=[pltpu.SMEM((8,), jnp.int32), pltpu.SemaphoreType.DMA((16,))],
        name="pack",
    )(place, keep, destination, *arrays)


def sort_kernel(source, *refs):
    pieces, out_ref = refs[:4], refs[4]
    for j in range(OUT_DEV):
        out_ref[pl.ds(j * ROWS, ROWS), :] = jnp.zeros((ROWS, TILE), jnp.bfloat16)
        for i in range(XS):

            @pl.when(source[j] == i)
            def _():
                out_ref[pl.ds(j * ROWS, ROWS), :] = pieces[i][1]


def sort_other(source, pieces):
    return pl.pallas_call(
        sort_kernel,
        out_shape=shaped((OUT_DEV * ROWS, TILE), jnp.bfloat16),
        in_specs=[SMEM] + [VMEM] * 4,
        out_specs=VMEM,
        name="sort",
    )(source, *pieces)


def unpack_kernel(source, *refs):
    pieces, swapped, x_ref, ss_ref = refs[:4], refs[4], refs[5], refs[6]
    ones = jnp.ones((8, TILE), jnp.float32)
    for j in range(OUT_DEV):
        rows = pl.ds(j * ROWS, ROWS)
        for i in range(XS):

            @pl.when(source[j] == i)
            def _():
                x_ref[rows, :] = pieces[i][0]

        @pl.when(source[j] == XS)
        def _():
            x_ref[rows, :] = swapped[rows, :]

        wide = x_ref[rows, :].astype(jnp.float32)
        sums = lax.dot_general(
            ones,
            wide * wide,
            (((1,), (1,)), ((), ())),
            precision=lax.Precision.HIGHEST,
            preferred_element_type=jnp.float32,
        )
        ss_ref[pl.ds(j, 1), :] = sums[0:1, :]


def unpack(source, pieces, swapped):
    return pl.pallas_call(
        unpack_kernel,
        out_shape=[
            shaped((OUT_DEV * ROWS, TILE), jnp.bfloat16),
            shaped((OUT_DEV, ROWS), jnp.float32),
        ],
        in_specs=[SMEM] + [VMEM] * 5,
        out_specs=[VMEM] * 2,
        name="unpack",
    )(source, *pieces, swapped)


SHARDS = 8
TOTAL = OUT_DEV * ROWS


def weight_block(weights, position, n):
    own, left, right, far_a, far_b = weights[5 * (position // 4) : 5 * (position // 4) + 5]
    if position % 4 < 3:
        return (own, left, right)[position % 4][n]
    return far_a[n] if n < 3 else far_b[n - 3]


def product(normed, rows, weights, n):
    total = None
    for p in range(SHARDS):
        term = jnp.dot(
            normed[rows, p * TILE : (p + 1) * TILE],
            weight_block(weights, p, n),
            preferred_element_type=jnp.float32,
        )
        total = term if total is None else total + term
    return total


def norm_kernel(meta, scale, gain, *refs):
    shards, weights = refs[:9], refs[9:19]
    normed, kv_ref = refs[19:21]

    def norm(src, rows, s):
        cols = pl.ds(pl.multiple_of(meta[8 + s] * TILE, TILE), TILE)
        normed[rows, cols] = (
            src[...].astype(jnp.float32) * scale[rows, :] * gain[pl.ds(meta[s], 1), :]
        ).astype(jnp.bfloat16)

    for s in range(7):
        norm(shards[s], pl.ds(0, TOTAL), s)
    norm(shards[7], pl.ds(0, TOTAL // 2), 7)
    norm(shards[8], pl.ds(TOTAL // 2, TOTAL // 2), 7)
    kv_ref[...] = product(normed, slice(0, TOTAL), weights, 4)


def norm_and_kv(meta, scale, gain, shards, weights):
    return pl.pallas_call(
        norm_kernel,
        out_shape=[
            shaped((TOTAL, SHARDS * TILE), jnp.bfloat16),
            shaped((TOTAL, TILE), jnp.float32),
        ],
        in_specs=[SMEM] + [VMEM] * 2 + [VMEM] * 9 + [VMEM] * 10,
        out_specs=[VMEM] * 2,
        cost_estimate=pl.CostEstimate(
            flops=2 * TOTAL * 2048 * 256, bytes_accessed=4 * 2**20, transcendentals=0
        ),
        name="norm_kv",
    )(meta, scale, gain, *shards, *weights)


def query_kernel(chunk, normed, *refs):
    weights = refs[:10]
    own_ref, others = refs[10], refs[11:14]
    rows = slice(chunk * TOTAL // 2, (chunk + 1) * TOTAL // 2)
    for n in (1, 2, 3):
        others[n - 1][...] = product(normed, rows, weights, n).astype(jnp.bfloat16)
    own_ref[...] = product(normed, rows, weights, 0)


def queries(chunk, normed, weights):
    half = TOTAL // 2
    return pl.pallas_call(
        functools.partial(query_kernel, chunk),
        out_shape=[shaped((half, TILE), jnp.float32)]
        + [shaped((half, TILE), jnp.bfloat16)] * 3,
        in_specs=[VMEM] * 11,
        out_specs=[VMEM] * 4,
        cost_estimate=pl.CostEstimate(
            flops=2 * half * 2048 * 1024, bytes_accessed=6 * 2**20, transcendentals=0
        ),
        name="queries",
    )(normed, *weights)


def attend_kernel(chunk, meta, own, o1, o2, o3, cosine, sine, fresh, *refs):
    caches, out_ref = refs[:8], refs[8]
    q = own[...] + o1[...].astype(jnp.float32) + o2[...].astype(jnp.float32)
    q = q + o3[...].astype(jnp.float32)
    turned = []
    for h in range(2):
        v = q[:, h * HEAD_SIZE : (h + 1) * HEAD_SIZE]
        turned.append((v * cosine[...] + swap_halves(v) * sine[...]).astype(jnp.bfloat16))
    wide_q = jnp.concatenate(turned, axis=0)
    valid = meta[2 * chunk + pl.program_id(0)]
    row = lax.broadcasted_iota(jnp.int32, (2 * ROWS, ROWS), 0) % ROWS
    column = lax.broadcasted_iota(jnp.int32, (2 * ROWS, ROWS), 1)
    allowed = (column <= row) & (column < valid)

    def score(keys):
        return lax.dot_general(
            wide_q, keys, (((1,), (1,)), ((), ())), preferred_element_type=jnp.float32
        ) * (HEAD_SIZE**-0.5)

    old = [score(cache[0, :, :HEAD_SIZE]) for cache in caches]
    new = jnp.where(allowed, score(fresh[0, :, :HEAD_SIZE]), MASKED_SCORE)
    top = jnp.maximum(
        jnp.max(functools.reduce(jnp.maximum, old), axis=1, keepdims=True),
        jnp.max(new, axis=1, keepdims=True),
    )
    old = [jnp.exp(v - top) for v in old]
    new = jnp.exp(new - top)
    total = jnp.sum(functools.reduce(jnp.add, old), axis=1, keepdims=True)
    total = total + jnp.sum(new, axis=1, keepdims=True)
    mixed = jnp.dot(
        new.astype(jnp.bfloat16), fresh[0, :, HEAD_SIZE:], preferred_element_type=jnp.float32
    )
    for v, cache in zip(old, caches):
        mixed = mixed + jnp.dot(
            v.astype(jnp.bfloat16), cache[0, :, HEAD_SIZE:], preferred_element_type=jnp.float32
        )
    mixed = jnp.where(row < valid, mixed / total, 0.0).astype(jnp.bfloat16)
    out_ref[0, :, :HEAD_SIZE] = mixed[:ROWS]
    out_ref[0, :, HEAD_SIZE:] = mixed[ROWS:]


def attend(chunk, meta, own, others, cosine, sine, fresh, caches, cache_blocks):
    by_slot = pl.BlockSpec((ROWS, TILE), lambda j, m: (j, 0))
    table = pl.BlockSpec((ROWS, HEAD_SIZE), lambda j, m: (0, 0))

    def cache_spec(block):
        return pl.BlockSpec((1, TILE, TILE), lambda j, m: (block, 0, 0))

    return pl.pallas_call(
        functools.partial(attend_kernel, chunk),
        out_shape=shaped((OUT_DEV // 2, ROWS, TILE), jnp.bfloat16),
        grid_spec=pltpu.PrefetchScalarGridSpec(
            num_scalar_prefetch=1,
            grid=(OUT_DEV // 2,),
            in_specs=[by_slot] * 4
            + [table] * 2
            + [pl.BlockSpec((1, ROWS, TILE), lambda j, m: (m[4 + 2 * chunk + j], 0, 0))]
            + [cache_spec(b) for b in cache_blocks],
            out_specs=pl.BlockSpec((1, ROWS, TILE), lambda j, m: (j, 0, 0)),
        ),
        cost_estimate=pl.CostEstimate(
            flops=4 * 512 * 2176 * 128, bytes_accessed=2 * 2**20, transcendentals=512 * 2176
        ),
        name="attend",
    )(meta, own, *others, cosine, sine, fresh, *caches)


def body(
    hidden,
    norm_gain,
    w_query,
    key_projection_weight,
    value_projection_weight,
    prompt_key_cache,
    prompt_value_cache,
    keep_flag,
    destination,
    row_counts,
):
    g = lax.axis_index("group")
    f = lax.axis_index("fsdp")
    x, c = g // CORES, g % CORES
    z, y = f // YS, f % YS
    tie = lax.optimization_barrier

    *pieces, part1, part2, part3, own_parts = pack(
        jnp.stack([x, c, z, y]).astype(jnp.int32),
        keep_flag,
        destination,
        hidden,
        w_query,
        key_projection_weight,
        value_projection_weight,
        prompt_key_cache,
        prompt_value_cache,
    )

    block_ids = jnp.arange(keep_flag.shape[0], dtype=jnp.int32)
    live = keep_flag == 1

    def slot_sources(core):
        slots = (x * CORES + core) * OUT_DEV + jnp.arange(OUT_DEV, dtype=jnp.int32)
        matched = live[None, :] & (destination[None, :] == slots[:, None])
        sources = jnp.sum(jnp.where(matched, block_ids[None, :], 0), axis=1)
        group = sources // IN_DEV
        distance = jnp.where(group % CORES == c, (x - group // CORES) % XS, XS)
        return distance.astype(jnp.int32), matched

    source_other, _ = slot_sources(1 - c)
    source_own, matched = slot_sources(c)
    lengths = jnp.sum(jnp.where(matched, row_counts[None, :], 0), axis=1)

    pieces = [pieces[0]] + [send_group(pieces[d], d, 0) for d in (1, 2, 3)]
    arrived = [send_y(part1, -1), send_y(part2, -2), send_y(part3, -3)]
    swapped = send_group(sort_other(source_other, pieces), 0, 1)
    rows, squares = unpack(source_own, pieces, swapped)

    own = jnp.concatenate([own_parts[:1], jnp.stack(arrived), own_parts[1:]], axis=0)

    def add_squares(value, bit):
        return value + lax.ppermute(value, "fsdp", [(i, i ^ bit) for i in range(ZS * YS)])

    left, right = send_group(own, 1, 0), send_group(own, -1, 0)
    fwd, bwd = [rows], [rows]

    def ring_step(squares, bit):
        a, b, squares = tie((fwd[-1], bwd[-1], squares))
        fwd.append(send_z(a, 1))
        bwd.append(send_z(b, -1))
        return add_squares(squares, bit)

    squares = ring_step(squares, 1)
    squares = ring_step(squares, 2)
    left, right, fwd[-1], bwd[-1] = tie((left, right, fwd[-1], bwd[-1]))
    far_a, far_b = send_group(left[:3], 1, 0), send_group(right[3:], -1, 0)
    squares = ring_step(squares, 4)
    a, b, squares = tie((fwd[3], bwd[3], squares))
    far = [send_z(a[: TOTAL // 2], 1), send_z(b[TOTAL // 2 :], -1)]
    squares = add_squares(squares, 8)
    squares = add_squares(squares, 16)
    scale = lax.rsqrt(squares / MODEL_WIDTH + EPSILON).reshape(TOTAL, 1)
    same_core = [own, left, right, far_a, far_b]
    other_core = [send_group(v, 0, 1) for v in same_core]
    weights = same_core + other_core

    shards = fwd[:4] + bwd[1:4] + far
    shard_ids = jnp.stack([(z + s) % ZS for s in (0, -1, -2, -3, 1, 2, 3, 4)])
    weight_ids = jnp.stack(
        [((x + dx) % XS) * CORES + cc for cc in (c, 1 - c) for dx in (0, -1, 1, 2)]
    )
    positions = jnp.sum(
        jnp.where(
            shard_ids[:, None] == weight_ids[None, :], jnp.arange(SHARDS, dtype=jnp.int32), 0
        ),
        axis=1,
    )
    gain = norm_gain.reshape(ZS, YS, TILE)
    gain = lax.dynamic_index_in_dim(gain, y, 1, keepdims=False).astype(jnp.float32)
    meta = jnp.concatenate([shard_ids, positions]).astype(jnp.int32)
    normed, kv_own = norm_and_kv(meta, scale, gain, shards, weights)

    kv_slots = kv_own.reshape(OUT_DEV, ROWS, TILE)
    kv_parts = [
        send_y(
            lax.dynamic_index_in_dim(kv_slots, (y + r) % YS, 0, keepdims=False).astype(
                jnp.bfloat16
            ),
            r,
        )
        for r in (1, 2, 3)
    ]
    kv = lax.dynamic_index_in_dim(kv_slots, y, 0, keepdims=False)
    for part in kv_parts:
        kv = kv + part.astype(jnp.float32)
    q_own0, *q_parts0 = queries(0, normed, weights)
    q_parts0 = [send_y(v, r) for r, v in zip((1, 2, 3), q_parts0)]
    q_own1, *q_parts1 = queries(1, normed, weights)
    q_parts1 = [send_y(v, r) for r, v in zip((1, 2, 3), q_parts1)]

    cosine, sine = rope_tables(ROWS, PROMPT_TOKENS)
    key = kv[:, :HEAD_SIZE]
    key = (key * cosine + swap_halves(key) * sine).astype(jnp.bfloat16)
    fresh_own = jnp.concatenate([key, kv[:, HEAD_SIZE:].astype(jnp.bfloat16)], axis=1)
    fresh = jnp.stack([fresh_own] + [send_y(fresh_own, r) for r in (1, 2, 3)])
    fresh_ids = (y - jnp.arange(OUT_DEV, dtype=jnp.int32)) % YS

    caches, cache_blocks = [], []
    for part in (same_core, other_core):
        caches += [part[0], part[1], part[2], part[4]]
        cache_blocks += [5, 5, 5, 2]
    meta = jnp.concatenate([lengths, fresh_ids]).astype(jnp.int32)
    tables = (cosine, sine, fresh, caches, cache_blocks)
    return jnp.concatenate(
        [
            attend(0, meta, q_own0, q_parts0, *tables),
            attend(1, meta, q_own1, q_parts1, *tables),
        ],
        axis=0,
    )


def solution(mesh):
    return jax.shard_map(
        body,
        mesh=mesh,
        in_specs=(
            P("group", None, "fsdp"),
            P(),
            P("group", "fsdp"),
            P("group", None),
            P("group", None),
            P("group", None),
            P("group", None),
            P(),
            P(),
            P(),
        ),
        out_specs=P("group", None, "fsdp"),
        check_vma=False,
    )
```

```python
import functools

import jax
import jax.numpy as jnp
from jax import lax
from jax.experimental import pallas as pl
from jax.experimental.pallas import tpu as pltpu
from jax.sharding import PartitionSpec as P

HEAD_SIZE = 128
PROMPT_TOKENS = 2048
IN_DEV = 8
OUT_DEV = 4
ROWS = 128
XS, CORES, ZS, YS = 4, 2, 8, 4
TILE = 256
MODEL_WIDTH = 8192

EPSILON = 1e-05
ROPE_THETA = 500000.0
CONTEXT_BASE = 8192.0
STRETCH = 8.0
MASKED_SCORE = -1e30

def group_perm(dx, dc):
    return [
        (x * CORES + c, ((x + dx) % XS) * CORES + (c ^ dc)) for x in range(XS) for c in range(CORES)
    ]


def z_perm(d):
    return [(z * YS + y, ((z + d) % ZS) * YS + y) for z in range(ZS) for y in range(YS)]


def y_perm(d):
    return [(z * YS + y, z * YS + (y + d) % YS) for z in range(ZS) for y in range(YS)]


def send_group(v, dx, dc):
    return lax.ppermute(v, "group", group_perm(dx, dc))


def send_z(v, d):
    return lax.ppermute(v, "fsdp", z_perm(d))


def send_y(v, d):
    return lax.ppermute(v, "fsdp", y_perm(d))


def swap(v):
    return send_group(v, 0, 1)


def rope_tables(length, offset):
    half_dim = HEAD_SIZE // 2
    base_rate = ROPE_THETA ** (-(jnp.arange(half_dim, dtype=jnp.float32) * 2.0 / HEAD_SIZE))
    ratio = CONTEXT_BASE * base_rate / (2.0 * jnp.pi)
    smooth = jnp.clip((ratio - 1.0) / 3.0, 0.0, 1.0)
    inverse_rate = (1.0 - smooth) * base_rate / STRETCH + smooth * base_rate
    token_positions = jnp.arange(length, dtype=jnp.float32) + offset
    angles = token_positions[:, None] * inverse_rate[None, :]
    cosine, sine = jnp.cos(angles), jnp.sin(angles)
    return (
        jnp.concatenate([cosine, cosine], axis=1),
        jnp.concatenate([-sine, sine], axis=1),
    )


def swap_halves(v):
    half = HEAD_SIZE // 2
    return jnp.concatenate([v[:, half:], v[:, :half]], axis=1)


ANY = pl.BlockSpec(memory_space=pl.ANY)
VMEM = pl.BlockSpec(memory_space=pltpu.VMEM)
SMEM = pl.BlockSpec(memory_space=pltpu.SMEM)


def shaped(shape, dtype):
    return jax.ShapeDtypeStruct(shape, dtype)


def limit(mib):
    return pltpu.CompilerParams(vmem_limit_bytes=mib * 2**20)


def fetch_all(pairs, sems, first=0):
    copies = [
        pltpu.make_async_copy(s, d, sems.at[first + i]) for i, (s, d) in enumerate(pairs)
    ]
    for copy in copies:
        copy.start()
    return copies


def await_all(copies):
    for copy in copies:
        copy.wait()


def pack_kernel(place, keep, destination, hidden, wq, wk, wv, kc, vc, *rest):
    outs, parts, own, chosen, sems = rest[0:4], rest[4:7], rest[7], rest[8], rest[9]
    x, c, z, y = place[0], place[1], place[2], place[3]
    first = (x * CORES + c) * IN_DEV
    cols = pl.ds(pl.multiple_of(z * HEAD_SIZE, HEAD_SIZE), HEAD_SIZE)
    rows = pl.ds(pl.multiple_of(y * TILE, TILE), TILE)
    pairs = []
    for r in range(1, 4):
        other = lax.rem(y + YS - r, YS)
        pairs.append((wq.at[pl.ds(pl.multiple_of(other * TILE, TILE), TILE)], parts[r - 1]))
    pairs.append((wq.at[rows], own.at[0]))
    pairs.append((wk.at[rows, cols], own.at[1, :, pl.ds(0, HEAD_SIZE)]))
    pairs.append((wv.at[rows, cols], own.at[1, :, pl.ds(HEAD_SIZE, HEAD_SIZE)]))
    pairs.append((kc.at[:, cols], own.at[2, :, pl.ds(0, HEAD_SIZE)]))
    pairs.append((vc.at[:, cols], own.at[2, :, pl.ds(HEAD_SIZE, HEAD_SIZE)]))
    copies = fetch_all(pairs, sems)

    for i in range(8):
        chosen[i] = 0
    for b in range(IN_DEV):

        @pl.when(keep[first + b] == 1)
        def _():
            target = lax.div(destination[first + b], OUT_DEV)
            dx = lax.rem(lax.div(target, CORES) + XS - x, XS)
            dc = lax.rem(target + c, CORES)
            chosen[dx * CORES + dc] = b

    pairs = [(hidden.at[chosen[i]], outs[i // CORES].at[i % CORES]) for i in range(8)]
    await_all(copies + fetch_all(pairs, sems, 8))


def pack(place, keep, destination, *arrays):
    bf16 = jnp.bfloat16
    return pl.pallas_call(
        pack_kernel,
        out_shape=[shaped((CORES, ROWS, TILE), bf16)] * 4
        + [shaped((TILE, TILE), bf16)] * 3
        + [shaped((3, TILE, TILE), bf16)],
        in_specs=[SMEM] * 3 + [ANY] * 6,
        out_specs=[VMEM] * 8,
        scratch_shapes=[pltpu.SMEM((8,), jnp.int32), pltpu.SemaphoreType.DMA((16,))],
        compiler_params=limit(56),
        name="pack",
    )(place, keep, destination, *arrays)


def plan_kernel(place, keep, destination, counts, out):
    x, c = place[0], place[1]

    def step(b, _):
        target = destination[b]
        group = lax.div(target, OUT_DEV)

        @pl.when((keep[b] == 1) & (lax.div(group, CORES) == x))
        def _():
            slot = lax.rem(target, OUT_DEV)
            source = lax.div(b, IN_DEV)
            other = lax.rem(group + c, CORES)
            dx = lax.rem(x + XS - lax.div(source, CORES), XS)
            out[other * OUT_DEV + slot] = jnp.where(lax.rem(source, CORES) == c, dx, XS)

            @pl.when(other == 0)
            def _():
                out[2 * OUT_DEV + slot] = counts[b]

        return 0

    lax.fori_loop(0, keep.shape[0], step, 0)


def plan(place, keep, destination, counts):
    return pl.pallas_call(
        plan_kernel,
        out_shape=shaped((3 * OUT_DEV,), jnp.int32),
        in_specs=[SMEM] * 4,
        out_specs=SMEM,
        compiler_params=limit(1),
        name="plan",
    )(place, keep, destination, counts)


SHARDS = 8
TOTAL = OUT_DEV * ROWS


def sort_kernel(source, *refs):
    pieces, own_ref, other_ref = refs[:4], refs[4], refs[5]
    for side, out_ref in ((0, own_ref), (1, other_ref)):
        for j in range(OUT_DEV):
            for i in range(XS):

                @pl.when(source[side * OUT_DEV + j] == i)
                def _():
                    out_ref[pl.ds(j * ROWS, ROWS), :] = pieces[i][side]


def sort_pieces(source, pieces):
    return pl.pallas_call(
        sort_kernel,
        out_shape=[shaped((TOTAL, TILE), jnp.bfloat16)] * 2,
        in_specs=[SMEM] + [VMEM] * 4,
        out_specs=[VMEM] * 2,
        compiler_params=limit(2),
        name="sort",
    )(source, *pieces)


def unpack_kernel(source, held, swapped, out_ref):
    for j in range(OUT_DEV):
        rows = pl.ds(j * ROWS, ROWS)
        there = source[j] == XS

        @pl.when(there)
        def _():
            out_ref[rows, :] = swapped[rows, :]

        @pl.when(jnp.logical_not(there))
        def _():
            out_ref[rows, :] = held[rows, :]


def unpack(source, held, swapped):
    return pl.pallas_call(
        unpack_kernel,
        out_shape=shaped((TOTAL, TILE), jnp.bfloat16),
        in_specs=[SMEM] + [VMEM] * 2,
        out_specs=VMEM,
        compiler_params=limit(2),
        name="unpack",
    )(source, held, swapped)


def squares_kernel(*refs):
    shards, out_ref = refs[:8], refs[8]
    total = None
    for shard in shards:
        wide = shard[...].astype(jnp.float32)
        total = wide * wide if total is None else total + wide * wide
    out_ref[...] = lax.dot_general(
        jnp.ones((8, TILE), jnp.float32),
        total,
        (((1,), (1,)), ((), ())),
        precision=lax.Precision.HIGHEST,
        preferred_element_type=jnp.float32,
    )


def sum_squares(shards):
    return pl.pallas_call(
        squares_kernel,
        out_shape=shaped((8, TOTAL), jnp.float32),
        in_specs=[VMEM] * 8,
        out_specs=VMEM,
        compiler_params=limit(2),
        name="squares",
    )(*shards)


SHARD_Z = (0, -1, -2, -3, 1, 2, 3, 4)


def product(normed, tiles, n):
    total = None
    for p in range(SHARDS):
        term = jnp.dot(
            normed[:, p * TILE : (p + 1) * TILE], tiles[p, n], preferred_element_type=jnp.float32
        )
        total = term if total is None else total + term
    return total


def project_kernel(place, s0, s1, s2, s3, gain, *refs):
    shards, weights = refs[:8], refs[8:18]
    own_ref, kv_ref, parts, cache_ref = refs[18], refs[19], refs[20:23], refs[23]
    held, tiles, normed, kv, own, sent, sems = refs[24:]
    x, c, z, y = place[0], place[1], place[2], place[3]
    copies = fetch_all([(shard, held.at[i]) for i, shard in enumerate(shards)], sems)
    pairs = []
    for half in range(2):
        base = 4 * half
        own_w, left, right, far_a, far_b = weights[5 * half : 5 * half + 5]
        for i, w in enumerate((own_w, left, right)):
            pairs.append((w, tiles.at[base + i]))
        pairs.append((far_a, tiles.at[base + 3, pl.ds(0, 3)]))
        pairs.append((far_b, tiles.at[base + 3, pl.ds(3, 3)]))
    fetched = fetch_all(pairs, sems, 8)
    sums = s0[...] + s1[...] + s2[...] + s3[...]
    scale = jnp.transpose(lax.rsqrt(sums / MODEL_WIDTH + EPSILON))[:, :1]
    for i, dz in enumerate(SHARD_Z):
        k = lax.rem(z + ZS + dz, ZS)
        ahead = lax.rem(lax.div(k, CORES) + XS - x, XS)
        order = jnp.where(ahead == 3, 1, jnp.where(ahead == 0, 0, ahead + 1))
        position = order + 4 * lax.rem(k + c, CORES)
        cols = pl.ds(pl.multiple_of(position * TILE, TILE), TILE)
        copies[i].wait()
        normed[:, cols] = (
            held[i].astype(jnp.float32) * scale * gain[pl.ds(k * YS + y, 1), :]
        ).astype(jnp.bfloat16)
    await_all(fetched)
    kv[...] = product(normed, tiles, 4)

    def slot(j):
        return kv.at[pl.ds(pl.multiple_of(j * ROWS, ROWS), ROWS)]

    outgoing = fetch_all([(slot(y), kv_ref)], sems, 18)
    outgoing += fetch_all(
        [(tiles.at[p, 5], cache_ref.at[pl.ds(p * TILE, TILE)]) for p in range(SHARDS)], sems, 23
    )
    for r in (1, 2, 3):
        sent[r - 1, pl.ds(TOTAL, ROWS), :] = slot(lax.rem(y + r, YS))[...].astype(jnp.bfloat16)
    for r in (2, 1, 3):
        sent[r - 1, pl.ds(0, TOTAL), :] = product(normed, tiles, r).astype(jnp.bfloat16)
        outgoing += fetch_all([(sent.at[r - 1], parts[r - 1])], sems, 18 + r)
    own[...] = product(normed, tiles, 0)
    outgoing += fetch_all([(own, own_ref)], sems, 22)
    await_all(outgoing)


def project(place, sums, gain, shards, weights):
    f32, bf16 = jnp.float32, jnp.bfloat16
    return pl.pallas_call(
        project_kernel,
        out_shape=[shaped((TOTAL, TILE), f32), shaped((ROWS, TILE), f32)]
        + [shaped((TOTAL + ROWS, TILE), bf16)] * 3
        + [shaped((PROMPT_TOKENS, TILE), bf16)],
        in_specs=[SMEM] + [VMEM] * 5 + [ANY] * 18,
        out_specs=[ANY] * 6,
        scratch_shapes=[
            pltpu.VMEM((SHARDS, TOTAL, TILE), bf16),
            pltpu.VMEM((SHARDS, 6, TILE, TILE), bf16),
            pltpu.VMEM((TOTAL, SHARDS * TILE), bf16),
            pltpu.VMEM((TOTAL, TILE), f32),
            pltpu.VMEM((TOTAL, TILE), f32),
            pltpu.VMEM((3, TOTAL + ROWS, TILE), bf16),
            pltpu.SemaphoreType.DMA((31,)),
        ],
        compiler_params=limit(56),
        cost_estimate=pl.CostEstimate(
            flops=2 * TOTAL * 2048 * 1280, bytes_accessed=10 * 2**20, transcendentals=0
        ),
        name="project",
    )(place, *sums, gain, *shards, *weights)


def rotate(v, cosine, sine):
    return v * cosine + swap_halves(v) * sine


def fresh_kernel(own_ref, p1, p2, p3, cosine, sine, out, held, own, sems):
    copies = fetch_all(
        [(p.at[pl.ds(TOTAL, ROWS)], held.at[i]) for i, p in enumerate((p1, p2, p3))], sems
    )
    await_all(fetch_all([(own_ref, own)], sems, 3))
    v = own[...]
    for i, copy in enumerate(copies):
        copy.wait()
        v = v + held[i].astype(jnp.float32)
    out[:, :HEAD_SIZE] = rotate(v[:, :HEAD_SIZE], cosine[...], sine[...]).astype(jnp.bfloat16)
    out[:, HEAD_SIZE:] = v[:, HEAD_SIZE:].astype(jnp.bfloat16)


def fresh_keys(own, parts, cosine, sine):
    return pl.pallas_call(
        fresh_kernel,
        out_shape=shaped((ROWS, TILE), jnp.bfloat16),
        in_specs=[ANY] * 4 + [VMEM] * 2,
        out_specs=VMEM,
        scratch_shapes=[
            pltpu.VMEM((3, ROWS, TILE), jnp.bfloat16),
            pltpu.VMEM((ROWS, TILE), jnp.float32),
            pltpu.SemaphoreType.DMA((4,)),
        ],
        compiler_params=limit(4),
        name="fresh",
    )(own, *parts, cosine, sine)


FACTOR = HEAD_SIZE**-0.5 * 1.4426950408889634


def prompt_kernel(own_ref, p1, p2, p3, cosine, sine, *refs):
    cache_ref, q_ref, mixed_ref, top_ref, total_ref = refs[:5]
    held, caches, own, sems = refs[5:]
    parts = fetch_all(
        [(p.at[pl.ds(0, TOTAL)], held.at[i]) for i, p in enumerate((p1, p2, p3))], sems
    )
    kept = fetch_all([(cache_ref, caches), (own_ref, own)], sems, 3)
    await_all(parts + kept)

    def step(j, _):
        rows = pl.ds(pl.multiple_of(j * ROWS, ROWS), ROWS)
        q = own[rows, :]
        for i in range(3):
            q = q + held[i, rows, :].astype(jnp.float32)
        halves = (q[:, :HEAD_SIZE], q[:, HEAD_SIZE:])
        wide_q = jnp.concatenate(
            [rotate(v, cosine[...], sine[...]).astype(jnp.bfloat16) for v in halves], axis=0
        )
        q_ref[j] = wide_q
        scores = [
            lax.dot_general(
                wide_q,
                caches[i * TILE : (i + 1) * TILE, :HEAD_SIZE],
                (((1,), (1,)), ((), ())),
                preferred_element_type=jnp.float32,
            )
            for i in range(8)
        ]
        top = jnp.max(functools.reduce(jnp.maximum, scores), axis=1, keepdims=True)
        scores = [jnp.exp2((v - top) * FACTOR) for v in scores]
        total = jnp.sum(functools.reduce(jnp.add, scores), axis=1, keepdims=True)
        mixed = None
        for i, v in enumerate(scores):
            term = jnp.dot(
                v.astype(jnp.bfloat16),
                caches[i * TILE : (i + 1) * TILE, HEAD_SIZE:],
                preferred_element_type=jnp.float32,
            )
            mixed = term if mixed is None else mixed + term
        mixed_ref[j] = mixed
        top_ref[j] = jnp.broadcast_to(top, (2 * ROWS, HEAD_SIZE))
        total_ref[j] = jnp.broadcast_to(total, (2 * ROWS, HEAD_SIZE))
        return 0

    lax.fori_loop(0, OUT_DEV, step, 0)


def attend_prompt(own, others, cosine, sine, cache):
    per_slot = (OUT_DEV, 2 * ROWS, HEAD_SIZE)
    return pl.pallas_call(
        prompt_kernel,
        out_shape=[shaped(per_slot, jnp.bfloat16)] + [shaped(per_slot, jnp.float32)] * 3,
        in_specs=[ANY] * 4 + [VMEM] * 2 + [ANY],
        out_specs=[VMEM] * 4,
        scratch_shapes=[
            pltpu.VMEM((3, TOTAL, TILE), jnp.bfloat16),
            pltpu.VMEM((PROMPT_TOKENS, TILE), jnp.bfloat16),
            pltpu.VMEM((TOTAL, TILE), jnp.float32),
            pltpu.SemaphoreType.DMA((5,)),
        ],
        compiler_params=limit(24),
        cost_estimate=pl.CostEstimate(
            flops=4 * 1024 * 2048 * 128, bytes_accessed=2 * 2**20, transcendentals=1024 * 2048
        ),
        name="prompt",
    )(own, *others, cosine, sine, cache)


def finish_kernel(place, slots, q, mixed_ref, top_ref, total_ref, f0, f1, f2, f3, out_ref, fresh):
    y = place[3]
    for r, part in enumerate((f0, f1, f2, f3)):
        fresh[lax.rem(y + YS - r, YS)] = part[...]
    row = lax.broadcasted_iota(jnp.int32, (2 * ROWS, ROWS), 0) % ROWS
    column = lax.broadcasted_iota(jnp.int32, (2 * ROWS, ROWS), 1)
    for j in range(OUT_DEV):
        valid = slots[2 * OUT_DEV + j]
        scores = lax.dot_general(
            q[j],
            fresh[j, :, :HEAD_SIZE],
            (((1,), (1,)), ((), ())),
            preferred_element_type=jnp.float32,
        )
        scores = jnp.where((column <= row) & (column < valid), scores, MASKED_SCORE)
        top = jnp.maximum(top_ref[j], jnp.max(scores, axis=1, keepdims=True))
        scores = jnp.exp2((scores - top) * FACTOR)
        rescale = jnp.exp2((top_ref[j] - top) * FACTOR)
        total = total_ref[j] * rescale + jnp.sum(scores, axis=1, keepdims=True)
        mixed = mixed_ref[j] * rescale + jnp.dot(
            scores.astype(jnp.bfloat16),
            fresh[j, :, HEAD_SIZE:],
            preferred_element_type=jnp.float32,
        )
        mixed = jnp.where(row < valid, mixed / total, 0.0).astype(jnp.bfloat16)
        out_ref[j, :, :HEAD_SIZE] = mixed[:ROWS]
        out_ref[j, :, HEAD_SIZE:] = mixed[ROWS:]


def finish(place, slots, prompt, fresh):
    return pl.pallas_call(
        finish_kernel,
        out_shape=shaped((OUT_DEV, ROWS, TILE), jnp.bfloat16),
        in_specs=[SMEM] * 2 + [VMEM] * 8,
        out_specs=VMEM,
        scratch_shapes=[pltpu.VMEM((OUT_DEV, ROWS, TILE), jnp.bfloat16)],
        compiler_params=limit(8),
        name="finish",
    )(place, slots, *prompt, *fresh)


def body(
    hidden,
    norm_gain,
    w_query,
    key_projection_weight,
    value_projection_weight,
    prompt_key_cache,
    prompt_value_cache,
    keep_flag,
    destination,
    row_counts,
):
    g = lax.axis_index("group")
    f = lax.axis_index("fsdp")
    place = jnp.stack([g // CORES, g % CORES, f // YS, f % YS]).astype(jnp.int32)
    tie = lax.optimization_barrier

    *pieces, part1, part2, part3, own_parts = pack(
        place,
        keep_flag,
        destination,
        hidden,
        w_query,
        key_projection_weight,
        value_projection_weight,
        prompt_key_cache,
        prompt_value_cache,
    )
    slots = plan(place, keep_flag, destination, row_counts)

    for d in (1, 3, 2):
        pieces[d] = send_group(pieces[d], d, 0)
    arrived = [send_y(part1, -1), send_y(part2, -2), send_y(part3, -3)]
    pieces, arrived = tie((pieces, arrived))
    inward, outward = sort_pieces(slots, pieces)
    swapped, arrived = tie((swap(outward), arrived))
    rows = unpack(slots, inward, swapped)

    own = jnp.concatenate([own_parts[:1], jnp.stack(arrived), own_parts[1:]], axis=0)
    f1, b1 = send_z(rows, 1), send_z(rows, -1)
    left, right = send_group(own, 1, 0), send_group(own, -1, 0)
    own_swapped = swap(own)
    f1, b1, own_swapped = tie((f1, b1, own_swapped))
    f2, b2 = send_z(f1, 1), send_z(b1, -1)
    f2, b2, left, right = tie((f2, b2, left, right))
    f3, b3 = send_z(f2, 1), send_z(b2, -1)
    far_a, far_b = send_group(left[:3], 1, 0), send_group(right[3:], -1, 0)
    left_swapped = swap(left)
    f3, b3, left_swapped, right = tie((f3, b3, left_swapped, right))
    far, right_swapped = send_z(f3, 1), swap(right)
    far, right_swapped, far_a, far_b = tie((far, right_swapped, far_a, far_b))
    shards = [rows, f1, f2, f3, b1, b2, b3, far]
    sums = sum_squares(shards)
    sums = [sums] + [send_y(sums, r) for r in (1, 2, 3)]
    same_core = [own, left, right, far_a, far_b]
    other_core = [own_swapped, left_swapped, right_swapped, swap(far_a), swap(far_b)]
    weights = same_core + other_core
    gain = norm_gain.astype(jnp.float32).reshape(ZS * YS, TILE)
    q_own, kv_own, *parts, cache = project(place, sums, gain, shards, weights)

    parts = [send_y(v, r) for r, v in zip((1, 2, 3), parts)]
    cosine, sine = rope_tables(ROWS, PROMPT_TOKENS)
    fresh = fresh_keys(kv_own, parts, cosine, sine)
    fresh = [fresh] + [send_y(fresh, r) for r in (1, 2, 3)]
    prompt = attend_prompt(q_own, parts, cosine, sine, cache)
    return finish(place, slots, prompt, fresh)


def solution(mesh):
    return jax.shard_map(
        body,
        mesh=mesh,
        in_specs=(
            P("group", None, "fsdp"),
            P(),
            P("group", "fsdp"),
            P("group", None),
            P("group", None),
            P("group", None),
            P("group", None),
            P(),
            P(),
            P(),
        ),
        out_specs=P("group", None, "fsdp"),
        check_vma=False,
    )
```

```python
import functools

import jax
import jax.numpy as jnp
from jax import lax
from jax.experimental import pallas as pl
from jax.experimental.pallas import tpu as pltpu
from jax.sharding import PartitionSpec as P

HEAD_SIZE = 128
PROMPT_TOKENS = 2048
IN_DEV = 8
OUT_DEV = 4
ROWS = 128
XS, CORES, ZS, YS = 4, 2, 8, 4
TILE = 256
MODEL_WIDTH = 8192

EPSILON = 1e-05
ROPE_THETA = 500000.0
CONTEXT_BASE = 8192.0
STRETCH = 8.0
MASKED_SCORE = -1e30

def other_of(a, r, size):
    return (a + (r if a % 2 == 0 else -r)) % size


def send_x(v, r):
    perm = [(x * CORES + c, other_of(x, r, XS) * CORES + c) for x in range(XS) for c in range(CORES)]
    return lax.ppermute(v, "group", perm)


def swap(v):
    return lax.ppermute(v, "group", [(g, g ^ 1) for g in range(XS * CORES)])


def send_z(v, r):
    perm = [(z * YS + y, other_of(z, r, ZS) * YS + y) for z in range(ZS) for y in range(YS)]
    return lax.ppermute(v, "fsdp", perm)


def send_y(v, r):
    perm = [(z * YS + y, z * YS + (y + r) % YS) for z in range(ZS) for y in range(YS)]
    return lax.ppermute(v, "fsdp", perm)


def relation(a, b):
    return lax.rem(4 + (1 - 2 * lax.rem(a, 2)) * (b - a), 4)


def rope_tables(length, offset):
    half_dim = HEAD_SIZE // 2
    base_rate = ROPE_THETA ** (-(jnp.arange(half_dim, dtype=jnp.float32) * 2.0 / HEAD_SIZE))
    ratio = CONTEXT_BASE * base_rate / (2.0 * jnp.pi)
    smooth = jnp.clip((ratio - 1.0) / 3.0, 0.0, 1.0)
    inverse_rate = (1.0 - smooth) * base_rate / STRETCH + smooth * base_rate
    token_positions = jnp.arange(length, dtype=jnp.float32) + offset
    angles = token_positions[:, None] * inverse_rate[None, :]
    cosine, sine = jnp.cos(angles), jnp.sin(angles)
    return (
        jnp.concatenate([cosine, cosine], axis=1),
        jnp.concatenate([-sine, sine], axis=1),
    )


def swap_halves(v):
    half = HEAD_SIZE // 2
    return jnp.concatenate([v[:, half:], v[:, :half]], axis=1)


ANY = pl.BlockSpec(memory_space=pl.ANY)
VMEM = pl.BlockSpec(memory_space=pltpu.VMEM)
SMEM = pl.BlockSpec(memory_space=pltpu.SMEM)


def shaped(shape, dtype):
    return jax.ShapeDtypeStruct(shape, dtype)


def limit(mib):
    return pltpu.CompilerParams(vmem_limit_bytes=mib * 2**20)


def fetch_all(pairs, sems, first=0):
    copies = [
        pltpu.make_async_copy(s, d, sems.at[first + i]) for i, (s, d) in enumerate(pairs)
    ]
    for copy in copies:
        copy.start()
    return copies


def await_all(copies):
    for copy in copies:
        copy.wait()


def pack_kernel(place, keep, destination, hidden, wq, wk, wv, kc, vc, *rest):
    outs, parts, own, chosen, sems = rest[0:4], rest[4:7], rest[7], rest[8], rest[9]
    x, c, z, y = place[0], place[1], place[2], place[3]
    first = (x * CORES + c) * IN_DEV
    cols = pl.ds(pl.multiple_of(z * HEAD_SIZE, HEAD_SIZE), HEAD_SIZE)
    rows = pl.ds(pl.multiple_of(y * TILE, TILE), TILE)
    pairs = []
    for r in range(1, 4):
        other = lax.rem(y + YS - r, YS)
        pairs.append((wq.at[pl.ds(pl.multiple_of(other * TILE, TILE), TILE)], parts[r - 1]))
    pairs.append((wq.at[rows], own.at[0]))
    pairs.append((wk.at[rows, cols], own.at[1, :, pl.ds(0, HEAD_SIZE)]))
    pairs.append((wv.at[rows, cols], own.at[1, :, pl.ds(HEAD_SIZE, HEAD_SIZE)]))
    pairs.append((kc.at[:, cols], own.at[2, :, pl.ds(0, HEAD_SIZE)]))
    pairs.append((vc.at[:, cols], own.at[2, :, pl.ds(HEAD_SIZE, HEAD_SIZE)]))
    copies = fetch_all(pairs, sems)

    for i in range(8):
        chosen[i] = 0
    for b in range(IN_DEV):

        @pl.when(keep[first + b] == 1)
        def _():
            target = lax.div(destination[first + b], OUT_DEV)
            dx = relation(x, lax.div(target, CORES))
            dc = lax.rem(target + c, CORES)
            chosen[dx * CORES + dc] = b

    pairs = [(hidden.at[chosen[i]], outs[i // CORES].at[i % CORES]) for i in range(8)]
    await_all(copies + fetch_all(pairs, sems, 8))


def pack(place, keep, destination, *arrays):
    bf16 = jnp.bfloat16
    return pl.pallas_call(
        pack_kernel,
        out_shape=[shaped((CORES, ROWS, TILE), bf16)] * 4
        + [shaped((TILE, TILE), bf16)] * 3
        + [shaped((3, TILE, TILE), bf16)],
        in_specs=[SMEM] * 3 + [ANY] * 6,
        out_specs=[VMEM] * 8,
        scratch_shapes=[pltpu.SMEM((8,), jnp.int32), pltpu.SemaphoreType.DMA((16,))],
        compiler_params=limit(56),
        name="pack",
    )(place, keep, destination, *arrays)


def plan_kernel(place, keep, destination, counts, piece, out, held):
    x, c = place[0], place[1]
    held[...] = piece[...]

    def step(b, _):
        target = destination[b]
        group = lax.div(target, OUT_DEV)

        @pl.when((keep[b] == 1) & (lax.div(group, CORES) == x))
        def _():
            slot = lax.rem(target, OUT_DEV)
            source = lax.div(b, IN_DEV)
            other = lax.rem(group + c, CORES)
            dx = relation(x, lax.div(source, CORES))
            out[other * OUT_DEV + slot] = jnp.where(lax.rem(source, CORES) == c, dx, XS)

            @pl.when(other == 0)
            def _():
                out[2 * OUT_DEV + slot] = counts[b]

        return 0

    lax.fori_loop(0, keep.shape[0], step, 0)


def plan(place, keep, destination, counts, piece):
    return pl.pallas_call(
        plan_kernel,
        out_shape=[shaped((3 * OUT_DEV,), jnp.int32), shaped(piece.shape, piece.dtype)],
        in_specs=[SMEM] * 4 + [VMEM],
        out_specs=[SMEM, VMEM],
        compiler_params=limit(1),
        name="plan",
    )(place, keep, destination, counts, piece)


SHARDS = 8
TOTAL = OUT_DEV * ROWS
EXTRA = 16


def sort_kernel(source, *refs):
    pieces, own_ref, other_ref = refs[:4], refs[4], refs[5]
    for side, out_ref in ((0, own_ref), (1, other_ref)):
        for j in range(OUT_DEV):
            for i in range(XS):

                @pl.when(source[side * OUT_DEV + j] == i)
                def _():
                    out_ref[pl.ds(j * ROWS, ROWS), :] = pieces[i][side]


def sort_pieces(source, pieces):
    return pl.pallas_call(
        sort_kernel,
        out_shape=[shaped((TOTAL, TILE), jnp.bfloat16)] * 2,
        in_specs=[SMEM] + [VMEM] * 4,
        out_specs=[VMEM] * 2,
        compiler_params=limit(2),
        name="sort",
    )(source, *pieces)


def unpack_kernel(source, held, swapped, x_ref, sums_ref):
    for j in range(OUT_DEV):
        rows = pl.ds(j * ROWS, ROWS)
        there = source[j] == XS

        @pl.when(there)
        def _():
            x_ref[rows, :] = swapped[rows, :]

        @pl.when(jnp.logical_not(there))
        def _():
            x_ref[rows, :] = held[rows, :]

    wide = x_ref[...].astype(jnp.float32)
    sums_ref[...] = lax.dot_general(
        jnp.ones((8, TILE), jnp.float32),
        wide * wide,
        (((1,), (1,)), ((), ())),
        precision=lax.Precision.HIGHEST,
        preferred_element_type=jnp.float32,
    )


def unpack(source, held, swapped):
    return pl.pallas_call(
        unpack_kernel,
        out_shape=[shaped((TOTAL, TILE), jnp.bfloat16), shaped((8, TOTAL), jnp.float32)],
        in_specs=[SMEM] + [VMEM] * 2,
        out_specs=[VMEM] * 2,
        compiler_params=limit(2),
        name="unpack",
    )(source, held, swapped)


def label_kernel(x, s0, s1, s2, s3, out):
    out[pl.ds(0, TOTAL), :] = x[...]
    value = s0[0:1, :] + s1[0:1, :] + s2[0:1, :] + s3[0:1, :]
    row = lax.broadcasted_iota(jnp.int32, (EXTRA, TILE), 0)
    table = jnp.zeros((EXTRA, TILE), jnp.float32)
    for term in range(3):
        rounded = value.astype(jnp.bfloat16).astype(jnp.float32)
        value = value - rounded
        for half in range(2):
            line = rounded[:, half * TILE : (half + 1) * TILE]
            table = jnp.where(row == 2 * term + half, line, table)
    out[pl.ds(TOTAL, EXTRA), :] = table.astype(jnp.bfloat16)


def label(x, sums):
    return pl.pallas_call(
        label_kernel,
        out_shape=shaped((TOTAL + EXTRA, TILE), jnp.bfloat16),
        in_specs=[VMEM] * 5,
        out_specs=VMEM,
        compiler_params=limit(4),
        name="label",
    )(x, *sums)


SHARD_Z = (0, 1, 2, 3, -1, -2, -3, 4)


def product(normed, tiles, n):
    total = None
    for p in range(SHARDS):
        term = jnp.dot(
            normed[:, p * TILE : (p + 1) * TILE], tiles[p, n], preferred_element_type=jnp.float32
        )
        total = term if total is None else total + term
    return total


def project_kernel(place, gain, *refs):
    shards, weights = refs[:8], refs[8:18]
    own_ref, parts, cache_ref = refs[18], refs[19:22], refs[22]
    held, tiles, normed, kv, own, sent, sems = refs[23:]
    x, c, z, y = place[0], place[1], place[2], place[3]
    copies = fetch_all([(shard, held.at[i]) for i, shard in enumerate(shards)], sems)
    pairs = []
    for half in range(2):
        base = 4 * half
        own_w, left, right, far_a, far_b = weights[5 * half : 5 * half + 5]
        for i, w in enumerate((own_w, left, right)):
            pairs.append((w, tiles.at[base + i]))
        pairs.append((far_a, tiles.at[base + 3, pl.ds(0, 3)]))
        pairs.append((far_b, tiles.at[base + 3, pl.ds(3, 3)]))
    fetched = fetch_all(pairs, sems, 8)
    await_all(copies)
    sums = functools.reduce(
        jnp.add, [held[i, TOTAL:, :].astype(jnp.float32) for i in range(SHARDS)]
    )
    scale = lax.rsqrt((sums[0:2] + sums[2:4] + sums[4:6]) / MODEL_WIDTH + EPSILON)
    scale = jnp.transpose(jnp.concatenate([scale] * 4, axis=0))
    scale = jnp.concatenate([scale[:, 0:1], scale[:, 1:2]], axis=0)
    for i, dz in enumerate(SHARD_Z):
        k = lax.rem(z + ZS + (1 - 2 * lax.rem(z, 2)) * dz, ZS)
        related = relation(x, lax.div(k, CORES))
        order = jnp.where(related >= 2, 5 - related, related)
        position = order + 4 * lax.rem(k + c, CORES)
        cols = pl.ds(pl.multiple_of(position * TILE, TILE), TILE)
        normed[:, cols] = (
            held[i, :TOTAL, :].astype(jnp.float32) * scale * gain[pl.ds(k * YS + y, 1), :]
        ).astype(jnp.bfloat16)
    await_all(fetched)
    kv[...] = product(normed, tiles, 4)

    def slot(j):
        return kv.at[pl.ds(pl.multiple_of(j * ROWS, ROWS), ROWS)]

    outgoing = fetch_all([(slot(y), own_ref.at[pl.ds(TOTAL, ROWS)])], sems, 18)
    outgoing += fetch_all(
        [(tiles.at[p, 5], cache_ref.at[pl.ds(p * TILE, TILE)]) for p in range(SHARDS)], sems, 23
    )
    for r in (1, 2, 3):
        sent[r - 1, pl.ds(TOTAL, ROWS), :] = slot(lax.rem(y + r, YS))[...].astype(jnp.bfloat16)
    for r in (2, 1, 3):
        sent[r - 1, pl.ds(0, TOTAL), :] = product(normed, tiles, r).astype(jnp.bfloat16)
        outgoing += fetch_all([(sent.at[r - 1], parts[r - 1])], sems, 18 + r)
    own[...] = product(normed, tiles, 0)
    outgoing += fetch_all([(own, own_ref.at[pl.ds(0, TOTAL)])], sems, 22)
    await_all(outgoing)


def project(place, gain, shards, weights):
    f32, bf16 = jnp.float32, jnp.bfloat16
    return pl.pallas_call(
        project_kernel,
        out_shape=[shaped((TOTAL + ROWS, TILE), f32)]
        + [shaped((TOTAL + ROWS, TILE), bf16)] * 3
        + [shaped((PROMPT_TOKENS, TILE), bf16)],
        in_specs=[SMEM, VMEM] + [ANY] * 18,
        out_specs=[ANY] * 5,
        scratch_shapes=[
            pltpu.VMEM((SHARDS, TOTAL + EXTRA, TILE), bf16),
            pltpu.VMEM((SHARDS, 6, TILE, TILE), bf16),
            pltpu.VMEM((TOTAL, SHARDS * TILE), bf16),
            pltpu.VMEM((TOTAL, TILE), f32),
            pltpu.VMEM((TOTAL, TILE), f32),
            pltpu.VMEM((3, TOTAL + ROWS, TILE), bf16),
            pltpu.SemaphoreType.DMA((31,)),
        ],
        compiler_params=limit(56),
        cost_estimate=pl.CostEstimate(
            flops=2 * TOTAL * 2048 * 1280, bytes_accessed=10 * 2**20, transcendentals=0
        ),
        name="project",
    )(place, gain, *shards, *weights)


def rotate(v, cosine, sine):
    return v * cosine + swap_halves(v) * sine


def fresh_kernel(own, p1, p2, p3, cosine, sine, out):
    v = own[...]
    for part in (p1, p2, p3):
        v = v + part[...].astype(jnp.float32)
    out[:, :HEAD_SIZE] = rotate(v[:, :HEAD_SIZE], cosine[...], sine[...]).astype(jnp.bfloat16)
    out[:, HEAD_SIZE:] = v[:, HEAD_SIZE:].astype(jnp.bfloat16)


def fresh_keys(own, parts, cosine, sine):
    last = pl.BlockSpec((ROWS, TILE), lambda i: (OUT_DEV, 0))
    table = pl.BlockSpec((ROWS, HEAD_SIZE), lambda i: (0, 0))
    return pl.pallas_call(
        fresh_kernel,
        out_shape=shaped((ROWS, TILE), jnp.bfloat16),
        grid=(1,),
        in_specs=[last] * 4 + [table] * 2,
        out_specs=pl.BlockSpec((ROWS, TILE), lambda i: (0, 0)),
        compiler_params=limit(4),
        name="fresh",
    )(own, *parts, cosine, sine)


FACTOR = HEAD_SIZE**-0.5 * 1.4426950408889634


def stage_kernel(own_ref, cache_ref, own, cache, sems):
    await_all(fetch_all([(own_ref, own), (cache_ref, cache)], sems))


def stage(own, cache):
    return pl.pallas_call(
        stage_kernel,
        out_shape=[shaped(own.shape, own.dtype), shaped(cache.shape, cache.dtype)],
        in_specs=[ANY] * 2,
        out_specs=[VMEM] * 2,
        scratch_shapes=[pltpu.SemaphoreType.DMA((2,))],
        compiler_params=limit(2),
        name="stage",
    )(own, cache)


def prompt_kernel(own, p1, p2, p3, cosine, sine, caches, q_ref, mixed_ref, top_ref, total_ref):
    def step(j, _):
        rows = pl.ds(pl.multiple_of(j * ROWS, ROWS), ROWS)
        q = own[rows, :]
        for part in (p1, p2, p3):
            q = q + part[rows, :].astype(jnp.float32)
        halves = (q[:, :HEAD_SIZE], q[:, HEAD_SIZE:])
        wide_q = jnp.concatenate(
            [rotate(v, cosine[...], sine[...]).astype(jnp.bfloat16) for v in halves], axis=0
        )
        q_ref[j] = wide_q
        scores = [
            lax.dot_general(
                wide_q,
                caches[i * TILE : (i + 1) * TILE, :HEAD_SIZE],
                (((1,), (1,)), ((), ())),
                preferred_element_type=jnp.float32,
            )
            for i in range(8)
        ]
        top = jnp.max(functools.reduce(jnp.maximum, scores), axis=1, keepdims=True)
        scores = [jnp.exp2((v - top) * FACTOR) for v in scores]
        total = jnp.sum(functools.reduce(jnp.add, scores), axis=1, keepdims=True)
        mixed = None
        for i, v in enumerate(scores):
            term = jnp.dot(
                v.astype(jnp.bfloat16),
                caches[i * TILE : (i + 1) * TILE, HEAD_SIZE:],
                preferred_element_type=jnp.float32,
            )
            mixed = term if mixed is None else mixed + term
        mixed_ref[j] = mixed
        top_ref[j] = jnp.broadcast_to(top, (2 * ROWS, HEAD_SIZE))
        total_ref[j] = jnp.broadcast_to(total, (2 * ROWS, HEAD_SIZE))
        return 0

    lax.fori_loop(0, OUT_DEV, step, 0)


def attend_prompt(own, others, cosine, sine, cache):
    per_slot = (OUT_DEV, 2 * ROWS, HEAD_SIZE)
    return pl.pallas_call(
        prompt_kernel,
        out_shape=[shaped(per_slot, jnp.bfloat16)] + [shaped(per_slot, jnp.float32)] * 3,
        in_specs=[VMEM] * 7,
        out_specs=[VMEM] * 4,
        compiler_params=limit(16),
        cost_estimate=pl.CostEstimate(
            flops=4 * 1024 * 2048 * 128, bytes_accessed=2 * 2**20, transcendentals=1024 * 2048
        ),
        name="prompt",
    )(own, *others, cosine, sine, cache)


def finish_kernel(place, slots, q, mixed_ref, top_ref, total_ref, f0, f1, f2, f3, out_ref, fresh):
    y = place[3]
    for r, part in enumerate((f0, f1, f2, f3)):
        fresh[lax.rem(y + YS - r, YS)] = part[...]
    row = lax.broadcasted_iota(jnp.int32, (2 * ROWS, ROWS), 0) % ROWS
    column = lax.broadcasted_iota(jnp.int32, (2 * ROWS, ROWS), 1)
    for j in range(OUT_DEV):
        valid = slots[2 * OUT_DEV + j]
        scores = lax.dot_general(
            q[j],
            fresh[j, :, :HEAD_SIZE],
            (((1,), (1,)), ((), ())),
            preferred_element_type=jnp.float32,
        )
        scores = jnp.where((column <= row) & (column < valid), scores, MASKED_SCORE)
        top = jnp.maximum(top_ref[j], jnp.max(scores, axis=1, keepdims=True))
        scores = jnp.exp2((scores - top) * FACTOR)
        rescale = jnp.exp2((top_ref[j] - top) * FACTOR)
        total = total_ref[j] * rescale + jnp.sum(scores, axis=1, keepdims=True)
        mixed = mixed_ref[j] * rescale + jnp.dot(
            scores.astype(jnp.bfloat16),
            fresh[j, :, HEAD_SIZE:],
            preferred_element_type=jnp.float32,
        )
        mixed = jnp.where(row < valid, mixed / total, 0.0).astype(jnp.bfloat16)
        out_ref[j, :, :HEAD_SIZE] = mixed[:ROWS]
        out_ref[j, :, HEAD_SIZE:] = mixed[ROWS:]


def finish(place, slots, prompt, fresh):
    return pl.pallas_call(
        finish_kernel,
        out_shape=shaped((OUT_DEV, ROWS, TILE), jnp.bfloat16),
        in_specs=[SMEM] * 2 + [VMEM] * 8,
        out_specs=VMEM,
        scratch_shapes=[pltpu.VMEM((OUT_DEV, ROWS, TILE), jnp.bfloat16)],
        compiler_params=limit(8),
        name="finish",
    )(place, slots, *prompt, *fresh)


def body(
    hidden,
    norm_gain,
    w_query,
    key_projection_weight,
    value_projection_weight,
    prompt_key_cache,
    prompt_value_cache,
    keep_flag,
    destination,
    row_counts,
):
    g = lax.axis_index("group")
    f = lax.axis_index("fsdp")
    place = jnp.stack([g // CORES, g % CORES, f // YS, f % YS]).astype(jnp.int32)
    tie = lax.optimization_barrier

    *pieces, part1, part2, part3, own_parts = pack(
        place,
        keep_flag,
        destination,
        hidden,
        w_query,
        key_projection_weight,
        value_projection_weight,
        prompt_key_cache,
        prompt_value_cache,
    )
    slots, pieces[0] = plan(place, keep_flag, destination, row_counts, pieces[0])

    for r in (1, 3, 2):
        pieces[r] = send_x(pieces[r], r)
    arrived = [send_y(part1, -1), send_y(part2, -2), send_y(part3, -3)]
    pieces, arrived = tie((pieces, arrived))
    inward, outward = sort_pieces(slots, pieces)
    rows, sums = unpack(slots, inward, swap(outward))
    sums = [sums] + [send_y(sums, r) for r in (1, 2, 3)]

    rows = label(rows, sums)
    rows, arrived = tie((rows, arrived))
    a1, b1 = send_z(rows, 1), send_z(rows, -1)
    own = jnp.concatenate([own_parts[:1], jnp.stack(arrived), own_parts[1:]], axis=0)
    near, next_ = send_x(own, 1), send_x(own, -1)
    own_swapped = swap(own)
    a1, b1, own_swapped = tie((a1, b1, own_swapped))
    a2, b2 = send_z(b1, 1), send_z(a1, -1)
    a2, b2, near, next_ = tie((a2, b2, near, next_))
    a3, b3 = send_z(b2, 1), send_z(a2, -1)
    far_a, far_b = send_x(next_[:3], 1), send_x(near[3:], -1)
    near_swapped = swap(near)
    a3, b3, far_a, far_b, near_swapped, next_ = tie((a3, b3, far_a, far_b, near_swapped, next_))
    far, next_swapped = send_z(b3, 1), swap(next_)
    far_a_swapped, far_b_swapped = swap(far_a), swap(far_b)
    shards = [rows, a1, a2, a3, b1, b2, b3, far]
    weights = [own, near, next_, far_a, far_b]
    weights += [own_swapped, near_swapped, next_swapped, far_a_swapped, far_b_swapped]
    gain = norm_gain.astype(jnp.float32).reshape(ZS * YS, TILE)
    q_own, *parts, cache = project(place, gain, shards, weights)

    parts = [send_y(v, r) for r, v in zip((1, 2, 3), parts)]
    q_own, cache = stage(q_own, cache)
    cosine, sine = rope_tables(ROWS, PROMPT_TOKENS)
    fresh = fresh_keys(q_own, parts, cosine, sine)
    fresh = [fresh] + [send_y(fresh, r) for r in (1, 2, 3)]
    prompt = attend_prompt(q_own, parts, cosine, sine, cache)
    return finish(place, slots, prompt, fresh)


def solution(mesh):
    return jax.shard_map(
        body,
        mesh=mesh,
        in_specs=(
            P("group", None, "fsdp"),
            P(),
            P("group", "fsdp"),
            P("group", None),
            P("group", None),
            P("group", None),
            P("group", None),
            P(),
            P(),
            P(),
        ),
        out_specs=P("group", None, "fsdp"),
        check_vma=False,
    )
```

```python
import functools

import jax
import jax.numpy as jnp
from jax import lax
from jax.experimental import pallas as pl
from jax.experimental.pallas import tpu as pltpu
from jax.sharding import PartitionSpec as P

HEAD_SIZE = 128
PROMPT_TOKENS = 2048
IN_DEV = 8
OUT_DEV = 4
ROWS = 128
XS, CORES, ZS, YS = 4, 2, 8, 4
TILE = 256
MODEL_WIDTH = 8192

EPSILON = 1e-05
ROPE_THETA = 500000.0
CONTEXT_BASE = 8192.0
STRETCH = 8.0
MASKED_SCORE = -1e30

def other_of(a, r, size):
    return (a + (r if a % 2 == 0 else -r)) % size


def send_x(v, r):
    perm = [(x * CORES + c, other_of(x, r, XS) * CORES + c) for x in range(XS) for c in range(CORES)]
    return lax.ppermute(v, "group", perm)


def swap(v):
    return lax.ppermute(v, "group", [(g, g ^ 1) for g in range(XS * CORES)])


def send_z(v, r):
    perm = [(z * YS + y, other_of(z, r, ZS) * YS + y) for z in range(ZS) for y in range(YS)]
    return lax.ppermute(v, "fsdp", perm)


def send_y(v, r):
    perm = [(z * YS + y, z * YS + (y + r) % YS) for z in range(ZS) for y in range(YS)]
    return lax.ppermute(v, "fsdp", perm)


def relation(a, b):
    return lax.rem(4 + (1 - 2 * lax.rem(a, 2)) * (b - a), 4)


def rope_tables(length, offset):
    half_dim = HEAD_SIZE // 2
    base_rate = ROPE_THETA ** (-(jnp.arange(half_dim, dtype=jnp.float32) * 2.0 / HEAD_SIZE))
    ratio = CONTEXT_BASE * base_rate / (2.0 * jnp.pi)
    smooth = jnp.clip((ratio - 1.0) / 3.0, 0.0, 1.0)
    inverse_rate = (1.0 - smooth) * base_rate / STRETCH + smooth * base_rate
    token_positions = jnp.arange(length, dtype=jnp.float32) + offset
    angles = token_positions[:, None] * inverse_rate[None, :]
    cosine, sine = jnp.cos(angles), jnp.sin(angles)
    return (
        jnp.concatenate([cosine, cosine], axis=1),
        jnp.concatenate([-sine, sine], axis=1),
    )


def swap_halves(v):
    half = HEAD_SIZE // 2
    return jnp.concatenate([v[:, half:], v[:, :half]], axis=1)


ANY = pl.BlockSpec(memory_space=pl.ANY)
VMEM = pl.BlockSpec(memory_space=pltpu.VMEM)
SMEM = pl.BlockSpec(memory_space=pltpu.SMEM)


def shaped(shape, dtype):
    return jax.ShapeDtypeStruct(shape, dtype)


def limit(mib):
    return pltpu.CompilerParams(vmem_limit_bytes=mib * 2**20)


def fetch_all(pairs, sems, first=0):
    copies = [
        pltpu.make_async_copy(s, d, sems.at[first + i]) for i, (s, d) in enumerate(pairs)
    ]
    for copy in copies:
        copy.start()
    return copies


def await_all(copies):
    for copy in copies:
        copy.wait()


def pack_kernel(keep, destination, hidden, wq, wk, wv, kc, vc, *rest):
    outs, parts, own, chosen, sems = rest[0:4], rest[4:7], rest[7], rest[8], rest[9]
    g, f = lax.axis_index("group"), lax.axis_index("fsdp")
    x, c, z, y = lax.div(g, CORES), lax.rem(g, CORES), lax.div(f, YS), lax.rem(f, YS)
    first = g * IN_DEV
    cols = pl.ds(pl.multiple_of(z * HEAD_SIZE, HEAD_SIZE), HEAD_SIZE)
    rows = pl.ds(pl.multiple_of(y * TILE, TILE), TILE)
    pairs = []
    for r in range(1, 4):
        other = lax.rem(y + YS - r, YS)
        pairs.append((wq.at[pl.ds(pl.multiple_of(other * TILE, TILE), TILE)], parts[r - 1]))
    pairs.append((wq.at[rows], own.at[0]))
    pairs.append((wk.at[rows, cols], own.at[1, :, pl.ds(0, HEAD_SIZE)]))
    pairs.append((wv.at[rows, cols], own.at[1, :, pl.ds(HEAD_SIZE, HEAD_SIZE)]))
    pairs.append((kc.at[:, cols], own.at[2, :, pl.ds(0, HEAD_SIZE)]))
    pairs.append((vc.at[:, cols], own.at[2, :, pl.ds(HEAD_SIZE, HEAD_SIZE)]))
    copies = fetch_all(pairs, sems)

    for i in range(8):
        chosen[i] = 0
    for b in range(IN_DEV):

        @pl.when(keep[first + b] == 1)
        def _():
            target = lax.div(destination[first + b], OUT_DEV)
            dx = relation(x, lax.div(target, CORES))
            dc = lax.rem(target + c, CORES)
            chosen[dx * CORES + dc] = b

    pairs = [(hidden.at[chosen[i]], outs[i // CORES].at[i % CORES]) for i in range(8)]
    await_all(copies + fetch_all(pairs, sems, 8))


def pack(keep, destination, *arrays):
    bf16 = jnp.bfloat16
    return pl.pallas_call(
        pack_kernel,
        out_shape=[shaped((CORES, ROWS, TILE), bf16)] * 4
        + [shaped((TILE, TILE), bf16)] * 3
        + [shaped((3, TILE, TILE), bf16)],
        in_specs=[SMEM] * 2 + [ANY] * 6,
        out_specs=[VMEM] * 8,
        scratch_shapes=[pltpu.SMEM((8,), jnp.int32), pltpu.SemaphoreType.DMA((16,))],
        compiler_params=limit(56),
        name="pack",
    )(keep, destination, *arrays)


def plan_kernel(place, keep, destination, counts, piece, out, held):
    x, c = place[0], place[1]
    held[...] = piece[...]

    def step(b, _):
        target = destination[b]
        group = lax.div(target, OUT_DEV)

        @pl.when((keep[b] == 1) & (lax.div(group, CORES) == x))
        def _():
            slot = lax.rem(target, OUT_DEV)
            source = lax.div(b, IN_DEV)
            other = lax.rem(group + c, CORES)
            dx = relation(x, lax.div(source, CORES))
            out[other * OUT_DEV + slot] = jnp.where(lax.rem(source, CORES) == c, dx, XS)

            @pl.when(other == 0)
            def _():
                out[2 * OUT_DEV + slot] = counts[b]

        return 0

    lax.fori_loop(0, keep.shape[0], step, 0)


def plan(place, keep, destination, counts, piece):
    return pl.pallas_call(
        plan_kernel,
        out_shape=[shaped((3 * OUT_DEV,), jnp.int32), shaped(piece.shape, piece.dtype)],
        in_specs=[SMEM] * 4 + [VMEM],
        out_specs=[SMEM, VMEM],
        compiler_params=limit(1),
        name="plan",
    )(place, keep, destination, counts, piece)


SHARDS = 8
TOTAL = OUT_DEV * ROWS
EXTRA = 16


def sort_kernel(source, *refs):
    pieces, own_ref, other_ref = refs[:4], refs[4], refs[5]
    for side, out_ref in ((0, own_ref), (1, other_ref)):
        for j in range(OUT_DEV):
            for i in range(XS):

                @pl.when(source[side * OUT_DEV + j] == i)
                def _():
                    out_ref[pl.ds(j * ROWS, ROWS), :] = pieces[i][side]


def sort_pieces(source, pieces):
    return pl.pallas_call(
        sort_kernel,
        out_shape=[shaped((TOTAL, TILE), jnp.bfloat16)] * 2,
        in_specs=[SMEM] + [VMEM] * 4,
        out_specs=[VMEM] * 2,
        compiler_params=limit(2),
        name="sort",
    )(source, *pieces)


def unpack_kernel(source, held, swapped, x_ref, sums_ref):
    for j in range(OUT_DEV):
        rows = pl.ds(j * ROWS, ROWS)
        there = source[j] == XS

        @pl.when(there)
        def _():
            x_ref[rows, :] = swapped[rows, :]

        @pl.when(jnp.logical_not(there))
        def _():
            x_ref[rows, :] = held[rows, :]

    wide = x_ref[...].astype(jnp.float32)
    sums_ref[...] = lax.dot_general(
        jnp.ones((8, TILE), jnp.float32),
        wide * wide,
        (((1,), (1,)), ((), ())),
        precision=lax.Precision.HIGHEST,
        preferred_element_type=jnp.float32,
    )


def unpack(source, held, swapped):
    return pl.pallas_call(
        unpack_kernel,
        out_shape=[shaped((TOTAL, TILE), jnp.bfloat16), shaped((8, TOTAL), jnp.float32)],
        in_specs=[SMEM] + [VMEM] * 2,
        out_specs=[VMEM] * 2,
        compiler_params=limit(2),
        name="unpack",
    )(source, held, swapped)


def label_kernel(x, s0, s1, s2, s3, out):
    out[pl.ds(0, TOTAL), :] = x[...]
    value = s0[0:1, :] + s1[0:1, :] + s2[0:1, :] + s3[0:1, :]
    row = lax.broadcasted_iota(jnp.int32, (EXTRA, TILE), 0)
    table = jnp.zeros((EXTRA, TILE), jnp.float32)
    for term in range(3):
        rounded = value.astype(jnp.bfloat16).astype(jnp.float32)
        value = value - rounded
        for half in range(2):
            line = rounded[:, half * TILE : (half + 1) * TILE]
            table = jnp.where(row == 2 * term + half, line, table)
    out[pl.ds(TOTAL, EXTRA), :] = table.astype(jnp.bfloat16)


def label(x, sums):
    return pl.pallas_call(
        label_kernel,
        out_shape=shaped((TOTAL + EXTRA, TILE), jnp.bfloat16),
        in_specs=[VMEM] * 5,
        out_specs=VMEM,
        compiler_params=limit(4),
        name="label",
    )(x, *sums)


SHARD_Z = (0, 1, 2, 3, -1, -2, -3, 4)


def product(normed, tiles, n):
    total = None
    for p in range(SHARDS):
        term = jnp.dot(
            normed[:, p * TILE : (p + 1) * TILE], tiles[p, n], preferred_element_type=jnp.float32
        )
        total = term if total is None else total + term
    return total


def project_kernel(place, gain, *refs):
    shards, weights = refs[:8], refs[8:18]
    own_ref, parts, cache_ref = refs[18], refs[19:22], refs[22]
    held, tiles, normed, kv, own, sent, sems = refs[23:]
    x, c, z, y = place[0], place[1], place[2], place[3]
    copies = fetch_all([(shard, held.at[i]) for i, shard in enumerate(shards)], sems)
    pairs = []
    for half in range(2):
        base = 4 * half
        own_w, left, right, far_a, far_b = weights[5 * half : 5 * half + 5]
        for i, w in enumerate((own_w, left, right)):
            pairs.append((w, tiles.at[base + i]))
        pairs.append((far_a, tiles.at[base + 3, pl.ds(0, 3)]))
        pairs.append((far_b, tiles.at[base + 3, pl.ds(3, 3)]))
    fetched = fetch_all(pairs, sems, 8)
    await_all(copies)
    sums = functools.reduce(
        jnp.add, [held[i, TOTAL:, :].astype(jnp.float32) for i in range(SHARDS)]
    )
    scale = lax.rsqrt((sums[0:2] + sums[2:4] + sums[4:6]) / MODEL_WIDTH + EPSILON)
    scale = jnp.transpose(jnp.concatenate([scale] * 4, axis=0))
    scale = jnp.concatenate([scale[:, 0:1], scale[:, 1:2]], axis=0)
    for i, dz in enumerate(SHARD_Z):
        k = lax.rem(z + ZS + (1 - 2 * lax.rem(z, 2)) * dz, ZS)
        related = relation(x, lax.div(k, CORES))
        order = jnp.where(related >= 2, 5 - related, related)
        position = order + 4 * lax.rem(k + c, CORES)
        cols = pl.ds(pl.multiple_of(position * TILE, TILE), TILE)
        normed[:, cols] = (
            held[i, :TOTAL, :].astype(jnp.float32) * scale * gain[pl.ds(k * YS + y, 1), :]
        ).astype(jnp.bfloat16)
    await_all(fetched)
    kv[...] = product(normed, tiles, 4)

    def slot(j):
        return kv.at[pl.ds(pl.multiple_of(j * ROWS, ROWS), ROWS)]

    outgoing = fetch_all([(slot(y), own_ref.at[pl.ds(TOTAL, ROWS)])], sems, 18)
    outgoing += fetch_all(
        [(tiles.at[p, 5], cache_ref.at[pl.ds(p * TILE, TILE)]) for p in range(SHARDS)], sems, 23
    )
    for r in (1, 2, 3):
        sent[r - 1, pl.ds(TOTAL, ROWS), :] = slot(lax.rem(y + r, YS))[...].astype(jnp.bfloat16)
    for r in (2, 1, 3):
        sent[r - 1, pl.ds(0, TOTAL), :] = product(normed, tiles, r).astype(jnp.bfloat16)
        outgoing += fetch_all([(sent.at[r - 1], parts[r - 1])], sems, 18 + r)
    own[...] = product(normed, tiles, 0)
    outgoing += fetch_all([(own, own_ref.at[pl.ds(0, TOTAL)])], sems, 22)
    await_all(outgoing)


def project(place, gain, shards, weights):
    f32, bf16 = jnp.float32, jnp.bfloat16
    return pl.pallas_call(
        project_kernel,
        out_shape=[shaped((TOTAL + ROWS, TILE), f32)]
        + [shaped((TOTAL + ROWS, TILE), bf16)] * 3
        + [shaped((PROMPT_TOKENS, TILE), bf16)],
        in_specs=[SMEM, VMEM] + [ANY] * 18,
        out_specs=[ANY] * 5,
        scratch_shapes=[
            pltpu.VMEM((SHARDS, TOTAL + EXTRA, TILE), bf16),
            pltpu.VMEM((SHARDS, 6, TILE, TILE), bf16),
            pltpu.VMEM((TOTAL, SHARDS * TILE), bf16),
            pltpu.VMEM((TOTAL, TILE), f32),
            pltpu.VMEM((TOTAL, TILE), f32),
            pltpu.VMEM((3, TOTAL + ROWS, TILE), bf16),
            pltpu.SemaphoreType.DMA((31,)),
        ],
        compiler_params=limit(56),
        cost_estimate=pl.CostEstimate(
            flops=2 * TOTAL * 2048 * 1280, bytes_accessed=10 * 2**20, transcendentals=0
        ),
        name="project",
    )(place, gain, *shards, *weights)


def rotate(v, cosine, sine):
    return v * cosine + swap_halves(v) * sine


def fresh_kernel(own, p1, p2, p3, cosine, sine, out):
    v = own[...]
    for part in (p1, p2, p3):
        v = v + part[...].astype(jnp.float32)
    out[:, :HEAD_SIZE] = rotate(v[:, :HEAD_SIZE], cosine[...], sine[...]).astype(jnp.bfloat16)
    out[:, HEAD_SIZE:] = v[:, HEAD_SIZE:].astype(jnp.bfloat16)


def fresh_keys(own, parts, cosine, sine):
    last = pl.BlockSpec((ROWS, TILE), lambda i: (OUT_DEV, 0))
    table = pl.BlockSpec((ROWS, HEAD_SIZE), lambda i: (0, 0))
    return pl.pallas_call(
        fresh_kernel,
        out_shape=shaped((ROWS, TILE), jnp.bfloat16),
        grid=(1,),
        in_specs=[last] * 4 + [table] * 2,
        out_specs=pl.BlockSpec((ROWS, TILE), lambda i: (0, 0)),
        compiler_params=limit(4),
        name="fresh",
    )(own, *parts, cosine, sine)


FACTOR = HEAD_SIZE**-0.5 * 1.4426950408889634


def stage_kernel(own_ref, cache_ref, own, cache, sems):
    await_all(fetch_all([(own_ref, own), (cache_ref, cache)], sems))


def stage(own, cache):
    return pl.pallas_call(
        stage_kernel,
        out_shape=[shaped(own.shape, own.dtype), shaped(cache.shape, cache.dtype)],
        in_specs=[ANY] * 2,
        out_specs=[VMEM] * 2,
        scratch_shapes=[pltpu.SemaphoreType.DMA((2,))],
        compiler_params=limit(2),
        name="stage",
    )(own, cache)


def prompt_kernel(own, p1, p2, p3, cosine, sine, caches, q_ref, mixed_ref, top_ref, total_ref):
    def step(j, _):
        rows = pl.ds(pl.multiple_of(j * ROWS, ROWS), ROWS)
        q = own[rows, :]
        for part in (p1, p2, p3):
            q = q + part[rows, :].astype(jnp.float32)
        halves = (q[:, :HEAD_SIZE], q[:, HEAD_SIZE:])
        wide_q = jnp.concatenate(
            [rotate(v, cosine[...], sine[...]).astype(jnp.bfloat16) for v in halves], axis=0
        )
        q_ref[j] = wide_q
        scores = [
            lax.dot_general(
                wide_q,
                caches[i * TILE : (i + 1) * TILE, :HEAD_SIZE],
                (((1,), (1,)), ((), ())),
                preferred_element_type=jnp.float32,
            )
            for i in range(8)
        ]
        top = jnp.max(functools.reduce(jnp.maximum, scores), axis=1, keepdims=True)
        scores = [jnp.exp2((v - top) * FACTOR) for v in scores]
        total = jnp.sum(functools.reduce(jnp.add, scores), axis=1, keepdims=True)
        mixed = None
        for i, v in enumerate(scores):
            term = jnp.dot(
                v.astype(jnp.bfloat16),
                caches[i * TILE : (i + 1) * TILE, HEAD_SIZE:],
                preferred_element_type=jnp.float32,
            )
            mixed = term if mixed is None else mixed + term
        mixed_ref[j] = mixed
        top_ref[j] = jnp.broadcast_to(top, (2 * ROWS, HEAD_SIZE))
        total_ref[j] = jnp.broadcast_to(total, (2 * ROWS, HEAD_SIZE))
        return 0

    lax.fori_loop(0, OUT_DEV, step, 0)


def attend_prompt(own, others, cosine, sine, cache):
    per_slot = (OUT_DEV, 2 * ROWS, HEAD_SIZE)
    return pl.pallas_call(
        prompt_kernel,
        out_shape=[shaped(per_slot, jnp.bfloat16)] + [shaped(per_slot, jnp.float32)] * 3,
        in_specs=[VMEM] * 7,
        out_specs=[VMEM] * 4,
        compiler_params=limit(16),
        cost_estimate=pl.CostEstimate(
            flops=4 * 1024 * 2048 * 128, bytes_accessed=2 * 2**20, transcendentals=1024 * 2048
        ),
        name="prompt",
    )(own, *others, cosine, sine, cache)


def finish_kernel(place, slots, q, mixed_ref, top_ref, total_ref, f0, f1, f2, f3, out_ref, fresh):
    y = place[3]
    for r, part in enumerate((f0, f1, f2, f3)):
        fresh[lax.rem(y + YS - r, YS)] = part[...]
    row = lax.broadcasted_iota(jnp.int32, (2 * ROWS, ROWS), 0) % ROWS
    column = lax.broadcasted_iota(jnp.int32, (2 * ROWS, ROWS), 1)
    for j in range(OUT_DEV):
        valid = slots[2 * OUT_DEV + j]
        scores = lax.dot_general(
            q[j],
            fresh[j, :, :HEAD_SIZE],
            (((1,), (1,)), ((), ())),
            preferred_element_type=jnp.float32,
        )
        scores = jnp.where((column <= row) & (column < valid), scores, MASKED_SCORE)
        top = jnp.maximum(top_ref[j], jnp.max(scores, axis=1, keepdims=True))
        scores = jnp.exp2((scores - top) * FACTOR)
        rescale = jnp.exp2((top_ref[j] - top) * FACTOR)
        total = total_ref[j] * rescale + jnp.sum(scores, axis=1, keepdims=True)
        mixed = mixed_ref[j] * rescale + jnp.dot(
            scores.astype(jnp.bfloat16),
            fresh[j, :, HEAD_SIZE:],
            preferred_element_type=jnp.float32,
        )
        mixed = jnp.where(row < valid, mixed / total, 0.0).astype(jnp.bfloat16)
        out_ref[j, :, :HEAD_SIZE] = mixed[:ROWS]
        out_ref[j, :, HEAD_SIZE:] = mixed[ROWS:]


def finish(place, slots, prompt, fresh):
    return pl.pallas_call(
        finish_kernel,
        out_shape=shaped((OUT_DEV, ROWS, TILE), jnp.bfloat16),
        in_specs=[SMEM] * 2 + [VMEM] * 8,
        out_specs=VMEM,
        scratch_shapes=[pltpu.VMEM((OUT_DEV, ROWS, TILE), jnp.bfloat16)],
        compiler_params=limit(8),
        name="finish",
    )(place, slots, *prompt, *fresh)


def body(
    hidden,
    norm_gain,
    w_query,
    key_projection_weight,
    value_projection_weight,
    prompt_key_cache,
    prompt_value_cache,
    keep_flag,
    destination,
    row_counts,
):
    g = lax.axis_index("group")
    f = lax.axis_index("fsdp")
    place = jnp.stack([g // CORES, g % CORES, f // YS, f % YS]).astype(jnp.int32)
    tie = lax.optimization_barrier

    *pieces, part1, part2, part3, own_parts = pack(
        keep_flag,
        destination,
        hidden,
        w_query,
        key_projection_weight,
        value_projection_weight,
        prompt_key_cache,
        prompt_value_cache,
    )

    for r in (1, 3, 2):
        pieces[r] = send_x(pieces[r], r)
    pieces[0], pieces[1] = tie((pieces[0], pieces[1]))
    slots, pieces[0] = plan(place, keep_flag, destination, row_counts, pieces[0])
    arrived = [send_y(part1, -1), send_y(part2, -2), send_y(part3, -3)]
    pieces, arrived = tie((pieces, arrived))
    inward, outward = sort_pieces(slots, pieces)
    rows, sums = unpack(slots, inward, swap(outward))
    sums = [sums] + [send_y(sums, r) for r in (1, 2, 3)]

    rows = label(rows, sums)
    own = jnp.concatenate([own_parts[:1], jnp.stack(arrived), own_parts[1:]], axis=0)
    near, next_ = send_x(own, 1), send_x(own, -1)
    rows, own = tie((rows, own))
    a1, b1, own_swapped = send_z(rows, 1), send_z(rows, -1), swap(own)
    a1, b1, own_swapped = tie((a1, b1, own_swapped))
    a2, b2 = send_z(b1, 1), send_z(a1, -1)
    a2, b2, near, next_ = tie((a2, b2, near, next_))
    a3, b3 = send_z(b2, 1), send_z(a2, -1)
    far_a, far_b = send_x(next_[:3], 1), send_x(near[3:], -1)
    a3, b3, far_a, far_b, near, next_ = tie((a3, b3, far_a, far_b, near, next_))
    far, near_swapped, next_swapped = send_z(b3, 1), swap(near), swap(next_)
    far_a_swapped, far_b_swapped = swap(far_a), swap(far_b)
    shards = [rows, a1, a2, a3, b1, b2, b3, far]
    weights = [own, near, next_, far_a, far_b]
    weights += [own_swapped, near_swapped, next_swapped, far_a_swapped, far_b_swapped]
    gain = norm_gain.astype(jnp.float32).reshape(ZS * YS, TILE)
    q_own, *parts, cache = project(place, gain, shards, weights)

    parts = [send_y(v, r) for r, v in zip((1, 2, 3), parts)]
    q_own, cache = stage(q_own, cache)
    cosine, sine = rope_tables(ROWS, PROMPT_TOKENS)
    fresh = fresh_keys(q_own, parts, cosine, sine)
    fresh = [fresh] + [send_y(fresh, r) for r in (1, 2, 3)]
    prompt = attend_prompt(q_own, parts, cosine, sine, cache)
    return finish(place, slots, prompt, fresh)


def solution(mesh):
    return jax.shard_map(
        body,
        mesh=mesh,
        in_specs=(
            P("group", None, "fsdp"),
            P(),
            P("group", "fsdp"),
            P("group", None),
            P("group", None),
            P("group", None),
            P("group", None),
            P(),
            P(),
            P(),
        ),
        out_specs=P("group", None, "fsdp"),
        check_vma=False,
    )
```

```python
import functools

import jax
import jax.numpy as jnp
from jax import lax
from jax.experimental import pallas as pl
from jax.experimental.pallas import tpu as pltpu
from jax.sharding import PartitionSpec as P

HEAD_SIZE = 128
PROMPT_TOKENS = 2048
IN_DEV = 8
OUT_DEV = 4
ROWS = 128
XS, CORES, ZS, YS = 4, 2, 8, 4
TILE = 256
MODEL_WIDTH = 8192

EPSILON = 1e-05
ROPE_THETA = 500000.0
CONTEXT_BASE = 8192.0
STRETCH = 8.0
MASKED_SCORE = -1e30

def other_of(a, r, size):
    return (a + (r if a % 2 == 0 else -r)) % size


def send_x(v, r):
    perm = [(x * CORES + c, other_of(x, r, XS) * CORES + c) for x in range(XS) for c in range(CORES)]
    return lax.ppermute(v, "group", perm)


def swap(v):
    return lax.ppermute(v, "group", [(g, g ^ 1) for g in range(XS * CORES)])


def send_z(v, r):
    perm = [(z * YS + y, other_of(z, r, ZS) * YS + y) for z in range(ZS) for y in range(YS)]
    return lax.ppermute(v, "fsdp", perm)


def send_y(v, r):
    perm = [(z * YS + y, z * YS + (y + r) % YS) for z in range(ZS) for y in range(YS)]
    return lax.ppermute(v, "fsdp", perm)


def relation(a, b):
    return lax.rem(4 + (1 - 2 * lax.rem(a, 2)) * (b - a), 4)


def rope_tables(length, offset):
    half_dim = HEAD_SIZE // 2
    base_rate = ROPE_THETA ** (-(jnp.arange(half_dim, dtype=jnp.float32) * 2.0 / HEAD_SIZE))
    ratio = CONTEXT_BASE * base_rate / (2.0 * jnp.pi)
    smooth = jnp.clip((ratio - 1.0) / 3.0, 0.0, 1.0)
    inverse_rate = (1.0 - smooth) * base_rate / STRETCH + smooth * base_rate
    token_positions = jnp.arange(length, dtype=jnp.float32) + offset
    angles = token_positions[:, None] * inverse_rate[None, :]
    cosine, sine = jnp.cos(angles), jnp.sin(angles)
    return (
        jnp.concatenate([cosine, cosine], axis=1),
        jnp.concatenate([-sine, sine], axis=1),
    )


def swap_halves(v):
    half = HEAD_SIZE // 2
    return jnp.concatenate([v[:, half:], v[:, :half]], axis=1)


ANY = pl.BlockSpec(memory_space=pl.ANY)
VMEM = pl.BlockSpec(memory_space=pltpu.VMEM)
SMEM = pl.BlockSpec(memory_space=pltpu.SMEM)


def shaped(shape, dtype):
    return jax.ShapeDtypeStruct(shape, dtype)


def limit(mib):
    return pltpu.CompilerParams(vmem_limit_bytes=mib * 2**20)


def fetch_all(pairs, sems, first=0):
    copies = [
        pltpu.make_async_copy(s, d, sems.at[first + i]) for i, (s, d) in enumerate(pairs)
    ]
    for copy in copies:
        copy.start()
    return copies


def await_all(copies):
    for copy in copies:
        copy.wait()


def pack_kernel(keep, destination, hidden, wq, wk, wv, kc, vc, *rest):
    outs, parts, own, chosen, sems = rest[0:4], rest[4:7], rest[7], rest[8], rest[9]
    g, f = lax.axis_index("group"), lax.axis_index("fsdp")
    x, c, z, y = lax.div(g, CORES), lax.rem(g, CORES), lax.div(f, YS), lax.rem(f, YS)
    first = g * IN_DEV
    cols = pl.ds(pl.multiple_of(z * HEAD_SIZE, HEAD_SIZE), HEAD_SIZE)
    rows = pl.ds(pl.multiple_of(y * TILE, TILE), TILE)
    pairs = []
    for r in range(1, 4):
        other = lax.rem(y + YS - r, YS)
        pairs.append((wq.at[pl.ds(pl.multiple_of(other * TILE, TILE), TILE)], parts[r - 1]))
    pairs.append((wq.at[rows], own.at[0]))
    pairs.append((wk.at[rows, cols], own.at[1, :, pl.ds(0, HEAD_SIZE)]))
    pairs.append((wv.at[rows, cols], own.at[1, :, pl.ds(HEAD_SIZE, HEAD_SIZE)]))
    pairs.append((kc.at[:, cols], own.at[2, :, pl.ds(0, HEAD_SIZE)]))
    pairs.append((vc.at[:, cols], own.at[2, :, pl.ds(HEAD_SIZE, HEAD_SIZE)]))
    copies = fetch_all(pairs, sems)

    for i in range(8):
        chosen[i] = 0
    for b in range(IN_DEV):

        @pl.when(keep[first + b] == 1)
        def _():
            target = lax.div(destination[first + b], OUT_DEV)
            dx = relation(x, lax.div(target, CORES))
            dc = lax.rem(target + c, CORES)
            chosen[dx * CORES + dc] = b

    pairs = [(hidden.at[chosen[i]], outs[i // CORES].at[i % CORES]) for i in range(8)]
    await_all(copies + fetch_all(pairs, sems, 8))


def pack(keep, destination, *arrays):
    bf16 = jnp.bfloat16
    return pl.pallas_call(
        pack_kernel,
        out_shape=[shaped((CORES, ROWS, TILE), bf16)] * 4
        + [shaped((TILE, TILE), bf16)] * 3
        + [shaped((3, TILE, TILE), bf16)],
        in_specs=[SMEM] * 2 + [ANY] * 6,
        out_specs=[VMEM] * 8,
        scratch_shapes=[pltpu.SMEM((8,), jnp.int32), pltpu.SemaphoreType.DMA((16,))],
        compiler_params=limit(56),
        name="pack",
    )(keep, destination, *arrays)


def plan_kernel(place, keep, destination, counts, piece, out, held):
    x, c = place[0], place[1]
    held[...] = piece[...]
    for chip in range(XS):
        dx = relation(x, chip)
        for core in range(CORES):
            found = jnp.where(c == core, dx, XS)
            for i in range(IN_DEV):
                b = (chip * CORES + core) * IN_DEV + i
                target = destination[b]
                slot = target & (OUT_DEV - 1)
                group = target >> 2
                other = (group ^ c) & 1
                here = (keep[b] == 1) & ((group >> 1) == x)
                out[jnp.where(here, other * OUT_DEV + slot, 3 * OUT_DEV)] = found
                mine = here & (other == 0)
                out[jnp.where(mine, 2 * OUT_DEV + slot, 3 * OUT_DEV + 1)] = counts[b]


def plan(place, keep, destination, counts, piece):
    return pl.pallas_call(
        plan_kernel,
        out_shape=[shaped((4 * OUT_DEV,), jnp.int32), shaped(piece.shape, piece.dtype)],
        in_specs=[SMEM] * 4 + [VMEM],
        out_specs=[SMEM, VMEM],
        compiler_params=limit(1),
        name="plan",
    )(place, keep, destination, counts, piece)


SHARDS = 8
TOTAL = OUT_DEV * ROWS
EXTRA = 16


def sort_kernel(source, *refs):
    pieces, own_ref, other_ref = refs[:4], refs[4], refs[5]
    for side, out_ref in ((0, own_ref), (1, other_ref)):
        for j in range(OUT_DEV):
            for i in range(XS):

                @pl.when(source[side * OUT_DEV + j] == i)
                def _():
                    out_ref[pl.ds(j * ROWS, ROWS), :] = pieces[i][side]


def sort_pieces(source, pieces):
    return pl.pallas_call(
        sort_kernel,
        out_shape=[shaped((TOTAL, TILE), jnp.bfloat16)] * 2,
        in_specs=[SMEM] + [VMEM] * 4,
        out_specs=[VMEM] * 2,
        compiler_params=limit(2),
        name="sort",
    )(source, *pieces)


def unpack_kernel(source, held, swapped, x_ref, sums_ref):
    for j in range(OUT_DEV):
        rows = pl.ds(j * ROWS, ROWS)
        there = source[j] == XS

        @pl.when(there)
        def _():
            x_ref[rows, :] = swapped[rows, :]

        @pl.when(jnp.logical_not(there))
        def _():
            x_ref[rows, :] = held[rows, :]

    wide = x_ref[...].astype(jnp.float32)
    sums_ref[...] = lax.dot_general(
        jnp.ones((8, TILE), jnp.float32),
        wide * wide,
        (((1,), (1,)), ((), ())),
        precision=lax.Precision.HIGHEST,
        preferred_element_type=jnp.float32,
    )


def unpack(source, held, swapped):
    return pl.pallas_call(
        unpack_kernel,
        out_shape=[shaped((TOTAL, TILE), jnp.bfloat16), shaped((8, TOTAL), jnp.float32)],
        in_specs=[SMEM] + [VMEM] * 2,
        out_specs=[VMEM] * 2,
        compiler_params=limit(2),
        name="unpack",
    )(source, held, swapped)


def label_kernel(x, s0, s1, s2, s3, out):
    out[pl.ds(0, TOTAL), :] = x[...]
    value = s0[0:1, :] + s1[0:1, :] + s2[0:1, :] + s3[0:1, :]
    row = lax.broadcasted_iota(jnp.int32, (EXTRA, TILE), 0)
    table = jnp.zeros((EXTRA, TILE), jnp.float32)
    for term in range(3):
        rounded = value.astype(jnp.bfloat16).astype(jnp.float32)
        value = value - rounded
        for half in range(2):
            line = rounded[:, half * TILE : (half + 1) * TILE]
            table = jnp.where(row == 2 * term + half, line, table)
    out[pl.ds(TOTAL, EXTRA), :] = table.astype(jnp.bfloat16)


def label(x, sums):
    return pl.pallas_call(
        label_kernel,
        out_shape=shaped((TOTAL + EXTRA, TILE), jnp.bfloat16),
        in_specs=[VMEM] * 5,
        out_specs=VMEM,
        compiler_params=limit(4),
        name="label",
    )(x, *sums)


SHARD_Z = (0, 1, 2, 3, -1, -2, -3, 4)


def block_copies(weights, tiles, start, count, sems, first):
    pairs = []
    for position in range(SHARDS):
        base, begin = 5 * (position // 4), start
        source = weights[base + position % 4] if position % 4 < 3 else weights[base + 3]
        if position % 4 == 3 and start >= 3:
            source, begin = weights[base + 4], start - 3
        pairs.append((source.at[pl.ds(begin, count)], tiles.at[position]))
    return fetch_all(pairs, sems, first)


def product(normed, tiles, n, copies=None):
    total = None
    for p in range(SHARDS):
        if copies is not None:
            copies[p].wait()
        term = jnp.dot(
            normed[:, p * TILE : (p + 1) * TILE], tiles[p, n], preferred_element_type=jnp.float32
        )
        total = term if total is None else total + term
    return total


def first_kernel(place, gain, *refs):
    shards, weights = refs[:8], refs[8:18]
    normed_ref, part_ref, kv_ref, kv_parts = refs[18:22]
    held, tiles, normed, kv, sent, small, sems = refs[22:]
    x, c, z, y = place[0], place[1], place[2], place[3]
    copies = fetch_all([(shard, held.at[i]) for i, shard in enumerate(shards)], sems)
    fetched = block_copies(weights, tiles, 3, 2, sems, 8)
    await_all(copies)
    sums = functools.reduce(
        jnp.add, [held[i, TOTAL:, :].astype(jnp.float32) for i in range(SHARDS)]
    )
    scale = lax.rsqrt((sums[0:2] + sums[2:4] + sums[4:6]) / MODEL_WIDTH + EPSILON)
    scale = jnp.transpose(jnp.concatenate([scale] * 4, axis=0))
    scale = jnp.concatenate([scale[:, 0:1], scale[:, 1:2]], axis=0)
    for i, dz in enumerate(SHARD_Z):
        k = lax.rem(z + ZS + (1 - 2 * lax.rem(z, 2)) * dz, ZS)
        related = relation(x, lax.div(k, CORES))
        order = jnp.where(related >= 2, 5 - related, related)
        position = order + 4 * lax.rem(k + c, CORES)
        cols = pl.ds(pl.multiple_of(position * TILE, TILE), TILE)
        normed[:, cols] = (
            held[i, :TOTAL, :].astype(jnp.float32) * scale * gain[pl.ds(k * YS + y, 1), :]
        ).astype(jnp.bfloat16)
    outgoing = fetch_all([(normed, normed_ref)], sems, 16)
    kv[...] = product(normed, tiles, 1, fetched)

    def slot(j):
        return kv.at[pl.ds(pl.multiple_of(j * ROWS, ROWS), ROWS)]

    sent[pl.ds(TOTAL, ROWS), :] = slot(lax.rem(y + 2, YS))[...].astype(jnp.bfloat16)
    for i, r in enumerate((1, 3)):
        small[i] = slot(lax.rem(y + r, YS))[...].astype(jnp.bfloat16)
    outgoing += fetch_all([(slot(y), kv_ref), (small, kv_parts)], sems, 17)
    sent[pl.ds(0, TOTAL), :] = product(normed, tiles, 0).astype(jnp.bfloat16)
    outgoing += fetch_all([(sent, part_ref)], sems, 19)
    await_all(outgoing)


def project_first(place, gain, shards, weights):
    f32, bf16 = jnp.float32, jnp.bfloat16
    return pl.pallas_call(
        first_kernel,
        out_shape=[
            shaped((TOTAL, SHARDS * TILE), bf16),
            shaped((TOTAL + ROWS, TILE), bf16),
            shaped((ROWS, TILE), f32),
            shaped((2, ROWS, TILE), bf16),
        ],
        in_specs=[SMEM, VMEM] + [ANY] * 18,
        out_specs=[ANY] * 4,
        scratch_shapes=[
            pltpu.VMEM((SHARDS, TOTAL + EXTRA, TILE), bf16),
            pltpu.VMEM((SHARDS, 2, TILE, TILE), bf16),
            pltpu.VMEM((TOTAL, SHARDS * TILE), bf16),
            pltpu.VMEM((TOTAL, TILE), f32),
            pltpu.VMEM((TOTAL + ROWS, TILE), bf16),
            pltpu.VMEM((2, ROWS, TILE), bf16),
            pltpu.SemaphoreType.DMA((20,)),
        ],
        compiler_params=limit(56),
        cost_estimate=pl.CostEstimate(
            flops=2 * TOTAL * 2048 * 512, bytes_accessed=6 * 2**20, transcendentals=0
        ),
        name="project_first",
    )(place, gain, *shards, *weights)


def second_kernel(normed_ref, kv_parts, *refs):
    weights, parts = refs[:10], refs[10:12]
    tiles, normed, sent, sems = refs[12:]
    rows = fetch_all([(normed_ref, normed)], sems)
    fetched = block_copies(weights, tiles, 1, 2, sems, 1)
    last = pl.ds(TOTAL, ROWS)
    small = fetch_all([(kv_parts.at[i], sent.at[i, last]) for i in range(2)], sems, 9)
    await_all(rows)
    outgoing = []
    for i in range(2):
        found = product(normed, tiles, i, fetched if i == 0 else None)
        sent[i, pl.ds(0, TOTAL), :] = found.astype(jnp.bfloat16)
        small[i].wait()
        outgoing += fetch_all([(sent.at[i], parts[i])], sems, 11 + i)
    await_all(outgoing)


def project_second(normed, kv_parts, weights):
    bf16 = jnp.bfloat16
    return pl.pallas_call(
        second_kernel,
        out_shape=[shaped((TOTAL + ROWS, TILE), bf16)] * 2,
        in_specs=[ANY] * 12,
        out_specs=[ANY] * 2,
        scratch_shapes=[
            pltpu.VMEM((SHARDS, 2, TILE, TILE), bf16),
            pltpu.VMEM((TOTAL, SHARDS * TILE), bf16),
            pltpu.VMEM((2, TOTAL + ROWS, TILE), bf16),
            pltpu.SemaphoreType.DMA((13,)),
        ],
        compiler_params=limit(56),
        cost_estimate=pl.CostEstimate(
            flops=2 * TOTAL * 2048 * 512, bytes_accessed=6 * 2**20, transcendentals=0
        ),
        name="project_second",
    )(normed, kv_parts, *weights)


def third_kernel(normed_ref, kv_ref, _, *refs):
    weights, own_ref = refs[:10], refs[10]
    tiles, normed, own, sems = refs[11:]
    rows = fetch_all([(normed_ref, normed)], sems)
    fetched = block_copies(weights, tiles, 0, 1, sems, 1)
    small = fetch_all([(kv_ref, own.at[pl.ds(TOTAL, ROWS)])], sems, 9)
    await_all(rows)
    own[pl.ds(0, TOTAL), :] = product(normed, tiles, 0, fetched)
    await_all(small)
    await_all(fetch_all([(own, own_ref)], sems, 10))


def project_third(normed, kv_own, after, weights):
    return pl.pallas_call(
        third_kernel,
        out_shape=shaped((TOTAL + ROWS, TILE), jnp.float32),
        in_specs=[ANY] * 13,
        out_specs=ANY,
        scratch_shapes=[
            pltpu.VMEM((SHARDS, 1, TILE, TILE), jnp.bfloat16),
            pltpu.VMEM((TOTAL, SHARDS * TILE), jnp.bfloat16),
            pltpu.VMEM((TOTAL + ROWS, TILE), jnp.float32),
            pltpu.SemaphoreType.DMA((11,)),
        ],
        compiler_params=limit(56),
        name="project_third",
    )(normed, kv_own, after, *weights)


def gather_kernel(*refs):
    weights, cache_ref, caches, sems = refs[:10], refs[10], refs[11], refs[12]
    outgoing = []
    for p, copy in enumerate(block_copies(weights, caches, 5, 1, sems, 0)):
        copy.wait()
        here = cache_ref.at[pl.ds(p * TILE, TILE)]
        outgoing += fetch_all([(caches.at[p, 0], here)], sems, SHARDS + p)
    await_all(outgoing)


def gather_cache(weights):
    return pl.pallas_call(
        gather_kernel,
        out_shape=shaped((PROMPT_TOKENS, TILE), jnp.bfloat16),
        in_specs=[ANY] * 10,
        out_specs=ANY,
        scratch_shapes=[
            pltpu.VMEM((SHARDS, 1, TILE, TILE), jnp.bfloat16),
            pltpu.SemaphoreType.DMA((2 * SHARDS,)),
        ],
        compiler_params=limit(56),
        name="gather",
    )(*weights)


def rotate(v, cosine, sine):
    return v * cosine + swap_halves(v) * sine


def fresh_kernel(own, p1, p3, cosine, sine, out):
    v = own[...]
    for part in (p1, p3):
        v = v + part[...].astype(jnp.float32)
    out[:, :HEAD_SIZE] = rotate(v[:, :HEAD_SIZE], cosine[...], sine[...]).astype(jnp.bfloat16)
    out[:, HEAD_SIZE:] = v[:, HEAD_SIZE:].astype(jnp.bfloat16)


def fresh_keys(own, parts, cosine, sine):
    last = pl.BlockSpec((ROWS, TILE), lambda i: (OUT_DEV, 0))
    table = pl.BlockSpec((ROWS, HEAD_SIZE), lambda i: (0, 0))
    return pl.pallas_call(
        fresh_kernel,
        out_shape=shaped((ROWS, TILE), jnp.bfloat16),
        grid=(1,),
        in_specs=[last] * 3 + [table] * 2,
        out_specs=pl.BlockSpec((ROWS, TILE), lambda i: (0, 0)),
        compiler_params=limit(4),
        name="fresh",
    )(own, *parts, cosine, sine)


FACTOR = HEAD_SIZE**-0.5 * 1.4426950408889634


def stage_kernel(own_ref, cache_ref, part, own, cache, sems):
    copies = fetch_all([(own_ref, own), (cache_ref, cache)], sems)
    copies[0].wait()
    own[...] += part[...].astype(jnp.float32)
    copies[1].wait()


def stage(own, cache, part):
    return pl.pallas_call(
        stage_kernel,
        out_shape=[shaped(own.shape, own.dtype), shaped(cache.shape, cache.dtype)],
        in_specs=[ANY] * 2 + [VMEM],
        out_specs=[VMEM] * 2,
        scratch_shapes=[pltpu.SemaphoreType.DMA((2,))],
        compiler_params=limit(2),
        name="stage",
    )(own, cache, part)


def prompt_kernel(own, p1, p3, cosine, sine, caches, q_ref, mixed_ref, top_ref, total_ref):
    def step(j, _):
        rows = pl.ds(pl.multiple_of(j * ROWS, ROWS), ROWS)
        q = own[rows, :]
        for part in (p1, p3):
            q = q + part[rows, :].astype(jnp.float32)
        halves = (q[:, :HEAD_SIZE], q[:, HEAD_SIZE:])
        wide_q = jnp.concatenate(
            [rotate(v, cosine[...], sine[...]).astype(jnp.bfloat16) for v in halves], axis=0
        )
        q_ref[j] = wide_q
        scores = [
            lax.dot_general(
                wide_q,
                caches[i * TILE : (i + 1) * TILE, :HEAD_SIZE],
                (((1,), (1,)), ((), ())),
                preferred_element_type=jnp.float32,
            )
            for i in range(8)
        ]
        top = jnp.max(functools.reduce(jnp.maximum, scores), axis=1, keepdims=True)
        scores = [jnp.exp2((v - top) * FACTOR) for v in scores]
        total = jnp.sum(functools.reduce(jnp.add, scores), axis=1, keepdims=True)
        mixed = None
        for i, v in enumerate(scores):
            term = jnp.dot(
                v.astype(jnp.bfloat16),
                caches[i * TILE : (i + 1) * TILE, HEAD_SIZE:],
                preferred_element_type=jnp.float32,
            )
            mixed = term if mixed is None else mixed + term
        mixed_ref[j] = mixed
        top_ref[j] = jnp.broadcast_to(top, (2 * ROWS, HEAD_SIZE))
        total_ref[j] = jnp.broadcast_to(total, (2 * ROWS, HEAD_SIZE))
        return 0

    lax.fori_loop(0, OUT_DEV, step, 0)


def attend_prompt(own, others, cosine, sine, cache):
    per_slot = (OUT_DEV, 2 * ROWS, HEAD_SIZE)
    return pl.pallas_call(
        prompt_kernel,
        out_shape=[shaped(per_slot, jnp.bfloat16)] + [shaped(per_slot, jnp.float32)] * 3,
        in_specs=[VMEM] * 6,
        out_specs=[VMEM] * 4,
        compiler_params=limit(16),
        cost_estimate=pl.CostEstimate(
            flops=4 * 1024 * 2048 * 128, bytes_accessed=2 * 2**20, transcendentals=1024 * 2048
        ),
        name="prompt",
    )(own, *others, cosine, sine, cache)


def finish_kernel(place, slots, q, mixed_ref, top_ref, total_ref, f0, f1, f2, f3, out_ref, fresh):
    y = place[3]
    for r, part in enumerate((f0, f1, f2, f3)):
        fresh[lax.rem(y + YS - r, YS)] = part[...]
    row = lax.broadcasted_iota(jnp.int32, (2 * ROWS, ROWS), 0) % ROWS
    column = lax.broadcasted_iota(jnp.int32, (2 * ROWS, ROWS), 1)
    for j in range(OUT_DEV):
        valid = slots[2 * OUT_DEV + j]
        scores = lax.dot_general(
            q[j],
            fresh[j, :, :HEAD_SIZE],
            (((1,), (1,)), ((), ())),
            preferred_element_type=jnp.float32,
        )
        scores = jnp.where((column <= row) & (column < valid), scores, MASKED_SCORE)
        top = jnp.maximum(top_ref[j], jnp.max(scores, axis=1, keepdims=True))
        scores = jnp.exp2((scores - top) * FACTOR)
        rescale = jnp.exp2((top_ref[j] - top) * FACTOR)
        total = total_ref[j] * rescale + jnp.sum(scores, axis=1, keepdims=True)
        mixed = mixed_ref[j] * rescale + jnp.dot(
            scores.astype(jnp.bfloat16),
            fresh[j, :, HEAD_SIZE:],
            preferred_element_type=jnp.float32,
        )
        mixed = jnp.where(row < valid, mixed / total, 0.0).astype(jnp.bfloat16)
        out_ref[j, :, :HEAD_SIZE] = mixed[:ROWS]
        out_ref[j, :, HEAD_SIZE:] = mixed[ROWS:]


def finish(place, slots, prompt, fresh):
    return pl.pallas_call(
        finish_kernel,
        out_shape=shaped((OUT_DEV, ROWS, TILE), jnp.bfloat16),
        in_specs=[SMEM] * 2 + [VMEM] * 8,
        out_specs=VMEM,
        scratch_shapes=[pltpu.VMEM((OUT_DEV, ROWS, TILE), jnp.bfloat16)],
        compiler_params=limit(8),
        name="finish",
    )(place, slots, *prompt, *fresh)


def body(
    hidden,
    norm_gain,
    w_query,
    key_projection_weight,
    value_projection_weight,
    prompt_key_cache,
    prompt_value_cache,
    keep_flag,
    destination,
    row_counts,
):
    g = lax.axis_index("group")
    f = lax.axis_index("fsdp")
    place = jnp.stack([g // CORES, g % CORES, f // YS, f % YS]).astype(jnp.int32)
    tie = lax.optimization_barrier

    *pieces, part1, part2, part3, own_parts = pack(
        keep_flag,
        destination,
        hidden,
        w_query,
        key_projection_weight,
        value_projection_weight,
        prompt_key_cache,
        prompt_value_cache,
    )

    for r in (1, 3, 2):
        pieces[r] = send_x(pieces[r], r)
    pieces[0], pieces[1] = tie((pieces[0], pieces[1]))
    slots, pieces[0] = plan(place, keep_flag, destination, row_counts, pieces[0])
    arrived = [send_y(part1, -1), send_y(part2, -2), send_y(part3, -3)]
    pieces, arrived[0] = tie((pieces, arrived[0]))
    inward, outward = sort_pieces(slots, pieces)
    rows, sums = unpack(slots, inward, swap(outward))
    sums = [sums] + [send_y(sums, r) for r in (1, 2, 3)]

    sums, arrived = tie((sums, arrived))
    rows = label(rows, sums)
    arrived = jnp.stack([arrived[0], arrived[2], arrived[1]])
    own = jnp.concatenate([own_parts[:1], arrived, own_parts[1:]], axis=0)
    near, next_ = send_x(own, 1), send_x(own, -1)
    rows, own = tie((rows, own))
    a1, b1, own_swapped = send_z(rows, 1), send_z(rows, -1), swap(own)
    a1, b1, own_swapped = tie((a1, b1, own_swapped))
    a2, b2 = send_z(b1, 1), send_z(a1, -1)
    a2, b2, near, next_ = tie((a2, b2, near, next_))
    a3, b3 = send_z(b2, 1), send_z(a2, -1)
    far_a, far_b = send_x(next_[:3], 1), send_x(near[3:], -1)
    a3, b3, far_a, far_b, near, next_ = tie((a3, b3, far_a, far_b, near, next_))
    far, near_swapped, next_swapped = send_z(b3, 1), swap(near), swap(next_)
    far_a_swapped, far_b_swapped = swap(far_a), swap(far_b)
    shards = [rows, a1, a2, a3, b1, b2, b3, far]
    weights = [own, near, next_, far_a, far_b]
    weights += [own_swapped, near_swapped, next_swapped, far_a_swapped, far_b_swapped]
    gain = norm_gain.astype(jnp.float32).reshape(ZS * YS, TILE)
    cache = gather_cache(weights)
    gain, cache = tie((gain, cache))
    normed, part2, kv_own, kv_parts = project_first(place, gain, shards, weights)
    part2 = send_y(part2, 2)
    part1, part3 = project_second(normed, kv_parts, weights)

    parts = [send_y(part1, 1), send_y(part3, 3)]
    q_own = project_third(normed, kv_own, part1, weights)
    q_own, cache = stage(q_own, cache, part2)
    cosine, sine = rope_tables(ROWS, PROMPT_TOKENS)
    fresh = fresh_keys(q_own, parts, cosine, sine)
    fresh = [fresh] + [send_y(fresh, r) for r in (1, 2, 3)]
    prompt = attend_prompt(q_own, parts, cosine, sine, cache)
    return finish(place, slots, prompt, fresh)


def solution(mesh):
    return jax.shard_map(
        body,
        mesh=mesh,
        in_specs=(
            P("group", None, "fsdp"),
            P(),
            P("group", "fsdp"),
            P("group", None),
            P("group", None),
            P("group", None),
            P("group", None),
            P(),
            P(),
            P(),
        ),
        out_specs=P("group", None, "fsdp"),
        check_vma=False,
    )
```

```python
import functools

import jax
import jax.numpy as jnp
from jax import lax
from jax.experimental import pallas as pl
from jax.experimental.pallas import tpu as pltpu
from jax.sharding import PartitionSpec as P

HEAD_SIZE = 128
PROMPT_TOKENS = 2048
IN_DEV = 8
OUT_DEV = 4
ROWS = 128
XS, CORES, ZS, YS = 4, 2, 8, 4
TILE = 256
MODEL_WIDTH = 8192

EPSILON = 1e-05
ROPE_THETA = 500000.0
CONTEXT_BASE = 8192.0
STRETCH = 8.0
MASKED_SCORE = -1e30

def other_of(a, r, size):
    return (a + (r if a % 2 == 0 else -r)) % size


def send_x(v, r):
    perm = [(x * CORES + c, other_of(x, r, XS) * CORES + c) for x in range(XS) for c in range(CORES)]
    return lax.ppermute(v, "group", perm)


def swap(v):
    return lax.ppermute(v, "group", [(g, g ^ 1) for g in range(XS * CORES)])


def send_z(v, r):
    perm = [(z * YS + y, other_of(z, r, ZS) * YS + y) for z in range(ZS) for y in range(YS)]
    return lax.ppermute(v, "fsdp", perm)


def send_y(v, r):
    perm = [(z * YS + y, z * YS + (y + r) % YS) for z in range(ZS) for y in range(YS)]
    return lax.ppermute(v, "fsdp", perm)


def relation(a, b):
    return lax.rem(4 + (1 - 2 * lax.rem(a, 2)) * (b - a), 4)


def rope_tables(length, offset):
    half_dim = HEAD_SIZE // 2
    base_rate = ROPE_THETA ** (-(jnp.arange(half_dim, dtype=jnp.float32) * 2.0 / HEAD_SIZE))
    ratio = CONTEXT_BASE * base_rate / (2.0 * jnp.pi)
    smooth = jnp.clip((ratio - 1.0) / 3.0, 0.0, 1.0)
    inverse_rate = (1.0 - smooth) * base_rate / STRETCH + smooth * base_rate
    token_positions = jnp.arange(length, dtype=jnp.float32) + offset
    angles = token_positions[:, None] * inverse_rate[None, :]
    cosine, sine = jnp.cos(angles), jnp.sin(angles)
    return (
        jnp.concatenate([cosine, cosine], axis=1),
        jnp.concatenate([-sine, sine], axis=1),
    )


def swap_halves(v):
    half = HEAD_SIZE // 2
    return jnp.concatenate([v[:, half:], v[:, :half]], axis=1)


ANY = pl.BlockSpec(memory_space=pl.ANY)
VMEM = pl.BlockSpec(memory_space=pltpu.VMEM)
SMEM = pl.BlockSpec(memory_space=pltpu.SMEM)


def shaped(shape, dtype):
    return jax.ShapeDtypeStruct(shape, dtype)


def limit(mib):
    return pltpu.CompilerParams(vmem_limit_bytes=mib * 2**20)


def fetch_all(pairs, sems, first=0):
    copies = [
        pltpu.make_async_copy(s, d, sems.at[first + i]) for i, (s, d) in enumerate(pairs)
    ]
    for copy in copies:
        copy.start()
    return copies


def await_all(copies):
    for copy in copies:
        copy.wait()


def pack_kernel(keep, destination, hidden, wq, wk, wv, kc, vc, *rest):
    outs, parts, own, chosen, sems = rest[0:4], rest[4:7], rest[7], rest[8], rest[9]
    g, f = lax.axis_index("group"), lax.axis_index("fsdp")
    x, c, z, y = lax.div(g, CORES), lax.rem(g, CORES), lax.div(f, YS), lax.rem(f, YS)
    first = g * IN_DEV
    cols = pl.ds(pl.multiple_of(z * HEAD_SIZE, HEAD_SIZE), HEAD_SIZE)
    rows = pl.ds(pl.multiple_of(y * TILE, TILE), TILE)
    pairs = []
    for r in range(1, 4):
        other = lax.rem(y + YS - r, YS)
        pairs.append((wq.at[pl.ds(pl.multiple_of(other * TILE, TILE), TILE)], parts[r - 1]))
    pairs.append((wq.at[rows], own.at[0]))
    pairs.append((wk.at[rows, cols], own.at[1, :, pl.ds(0, HEAD_SIZE)]))
    pairs.append((wv.at[rows, cols], own.at[1, :, pl.ds(HEAD_SIZE, HEAD_SIZE)]))
    pairs.append((kc.at[:, cols], own.at[2, :, pl.ds(0, HEAD_SIZE)]))
    pairs.append((vc.at[:, cols], own.at[2, :, pl.ds(HEAD_SIZE, HEAD_SIZE)]))
    copies = fetch_all(pairs, sems)

    for i in range(8):
        chosen[i] = 0
    for b in range(IN_DEV):

        @pl.when(keep[first + b] == 1)
        def _():
            target = lax.div(destination[first + b], OUT_DEV)
            dx = relation(x, lax.div(target, CORES))
            dc = lax.rem(target + c, CORES)
            chosen[dx * CORES + dc] = b

    pairs = [(hidden.at[chosen[i]], outs[i // CORES].at[i % CORES]) for i in range(8)]
    await_all(copies + fetch_all(pairs, sems, 8))


def pack(keep, destination, *arrays):
    bf16 = jnp.bfloat16
    return pl.pallas_call(
        pack_kernel,
        out_shape=[shaped((CORES, ROWS, TILE), bf16)] * 4
        + [shaped((TILE, TILE), bf16)] * 3
        + [shaped((3, TILE, TILE), bf16)],
        in_specs=[SMEM] * 2 + [ANY] * 6,
        out_specs=[VMEM] * 8,
        scratch_shapes=[pltpu.SMEM((8,), jnp.int32), pltpu.SemaphoreType.DMA((16,))],
        compiler_params=limit(56),
        name="pack",
    )(keep, destination, *arrays)


def plan_kernel(place, keep, destination, counts, piece, out, held):
    x, c = place[0], place[1]
    held[...] = piece[...]
    for chip in range(XS):
        dx = relation(x, chip)
        for core in range(CORES):
            found = jnp.where(c == core, dx, XS)
            for i in range(IN_DEV):
                b = (chip * CORES + core) * IN_DEV + i
                target = destination[b]
                slot = target & (OUT_DEV - 1)
                group = target >> 2
                other = (group ^ c) & 1
                here = (keep[b] == 1) & ((group >> 1) == x)
                out[jnp.where(here, other * OUT_DEV + slot, 3 * OUT_DEV)] = found
                mine = here & (other == 0)
                out[jnp.where(mine, 2 * OUT_DEV + slot, 3 * OUT_DEV + 1)] = counts[b]


def plan(place, keep, destination, counts, piece):
    return pl.pallas_call(
        plan_kernel,
        out_shape=[shaped((4 * OUT_DEV,), jnp.int32), shaped(piece.shape, piece.dtype)],
        in_specs=[SMEM] * 4 + [VMEM],
        out_specs=[SMEM, VMEM],
        compiler_params=limit(1),
        name="plan",
    )(place, keep, destination, counts, piece)


SHARDS = 8
TOTAL = OUT_DEV * ROWS
EXTRA = 16


def sort_kernel(source, *refs):
    pieces, own_ref, other_ref = refs[:4], refs[4], refs[5]
    for side, out_ref in ((0, own_ref), (1, other_ref)):
        for j in range(OUT_DEV):
            for i in range(XS):

                @pl.when(source[side * OUT_DEV + j] == i)
                def _():
                    out_ref[pl.ds(j * ROWS, ROWS), :] = pieces[i][side]


def sort_pieces(source, pieces):
    return pl.pallas_call(
        sort_kernel,
        out_shape=[shaped((TOTAL, TILE), jnp.bfloat16)] * 2,
        in_specs=[SMEM] + [VMEM] * 4,
        out_specs=[VMEM] * 2,
        compiler_params=limit(2),
        name="sort",
    )(source, *pieces)


def unpack_kernel(source, held, swapped, x_ref, sums_ref):
    for j in range(OUT_DEV):
        rows = pl.ds(j * ROWS, ROWS)
        there = source[j] == XS

        @pl.when(there)
        def _():
            x_ref[rows, :] = swapped[rows, :]

        @pl.when(jnp.logical_not(there))
        def _():
            x_ref[rows, :] = held[rows, :]

    wide = x_ref[...].astype(jnp.float32)
    sums_ref[...] = lax.dot_general(
        jnp.ones((8, TILE), jnp.float32),
        wide * wide,
        (((1,), (1,)), ((), ())),
        precision=lax.Precision.HIGHEST,
        preferred_element_type=jnp.float32,
    )


def unpack(source, held, swapped):
    return pl.pallas_call(
        unpack_kernel,
        out_shape=[shaped((TOTAL, TILE), jnp.bfloat16), shaped((8, TOTAL), jnp.float32)],
        in_specs=[SMEM] + [VMEM] * 2,
        out_specs=[VMEM] * 2,
        compiler_params=limit(2),
        name="unpack",
    )(source, held, swapped)


def label_kernel(x, s0, s1, s2, s3, out):
    out[pl.ds(0, TOTAL), :] = x[...]
    value = s0[0:1, :] + s1[0:1, :] + s2[0:1, :] + s3[0:1, :]
    row = lax.broadcasted_iota(jnp.int32, (EXTRA, TILE), 0)
    table = jnp.zeros((EXTRA, TILE), jnp.float32)
    for term in range(3):
        rounded = value.astype(jnp.bfloat16).astype(jnp.float32)
        value = value - rounded
        for half in range(2):
            line = rounded[:, half * TILE : (half + 1) * TILE]
            table = jnp.where(row == 2 * term + half, line, table)
    out[pl.ds(TOTAL, EXTRA), :] = table.astype(jnp.bfloat16)


def label(x, sums):
    return pl.pallas_call(
        label_kernel,
        out_shape=shaped((TOTAL + EXTRA, TILE), jnp.bfloat16),
        in_specs=[VMEM] * 5,
        out_specs=VMEM,
        compiler_params=limit(4),
        name="label",
    )(x, *sums)


SHARD_Z = (0, 1, 2, 3, -1, -2, -3, 4)


def block_copies(weights, tiles, start, count, sems, first):
    pairs = []
    for position in range(SHARDS):
        base, begin = 5 * (position // 4), start
        source = weights[base + position % 4] if position % 4 < 3 else weights[base + 3]
        if position % 4 == 3 and start >= 3:
            source, begin = weights[base + 4], start - 3
        pairs.append((source.at[pl.ds(begin, count)], tiles.at[position]))
    return fetch_all(pairs, sems, first)


def product(normed, tiles, n, copies=None):
    total = None
    for p in range(SHARDS):
        if copies is not None:
            copies[p].wait()
        term = jnp.dot(
            normed[:, p * TILE : (p + 1) * TILE], tiles[p, n], preferred_element_type=jnp.float32
        )
        total = term if total is None else total + term
    return total


def first_kernel(place, gain, *refs):
    shards, weights = refs[:8], refs[8:18]
    normed_ref, part_ref, kv_ref, kv_parts = refs[18:22]
    held, tiles, normed, kv, sent, small, sems = refs[22:]
    x, c, z, y = place[0], place[1], place[2], place[3]
    copies = fetch_all([(shard, held.at[i]) for i, shard in enumerate(shards)], sems)
    fetched = block_copies(weights, tiles, 3, 2, sems, 8)
    await_all(copies)
    sums = functools.reduce(
        jnp.add, [held[i, TOTAL:, :].astype(jnp.float32) for i in range(SHARDS)]
    )
    scale = lax.rsqrt((sums[0:2] + sums[2:4] + sums[4:6]) / MODEL_WIDTH + EPSILON)
    scale = jnp.transpose(jnp.concatenate([scale] * 4, axis=0))
    scale = jnp.concatenate([scale[:, 0:1], scale[:, 1:2]], axis=0)
    for i, dz in enumerate(SHARD_Z):
        k = lax.rem(z + ZS + (1 - 2 * lax.rem(z, 2)) * dz, ZS)
        related = relation(x, lax.div(k, CORES))
        order = jnp.where(related >= 2, 5 - related, related)
        position = order + 4 * lax.rem(k + c, CORES)
        cols = pl.ds(pl.multiple_of(position * TILE, TILE), TILE)
        normed[:, cols] = (
            held[i, :TOTAL, :].astype(jnp.float32) * scale * gain[pl.ds(k * YS + y, 1), :]
        ).astype(jnp.bfloat16)
    outgoing = fetch_all([(normed, normed_ref)], sems, 16)
    kv[...] = product(normed, tiles, 1, fetched)

    def slot(j):
        return kv.at[pl.ds(pl.multiple_of(j * ROWS, ROWS), ROWS)]

    sent[pl.ds(TOTAL, ROWS), :] = slot(lax.rem(y + 2, YS))[...].astype(jnp.bfloat16)
    for i, r in enumerate((1, 3)):
        small[i] = slot(lax.rem(y + r, YS))[...].astype(jnp.bfloat16)
    outgoing += fetch_all([(slot(y), kv_ref), (small, kv_parts)], sems, 17)
    sent[pl.ds(0, TOTAL), :] = product(normed, tiles, 0).astype(jnp.bfloat16)
    outgoing += fetch_all([(sent, part_ref)], sems, 19)
    await_all(outgoing)


def project_first(place, gain, shards, weights):
    f32, bf16 = jnp.float32, jnp.bfloat16
    return pl.pallas_call(
        first_kernel,
        out_shape=[
            shaped((TOTAL, SHARDS * TILE), bf16),
            shaped((TOTAL + ROWS, TILE), bf16),
            shaped((ROWS, TILE), f32),
            shaped((2, ROWS, TILE), bf16),
        ],
        in_specs=[SMEM, VMEM] + [ANY] * 18,
        out_specs=[ANY] * 4,
        scratch_shapes=[
            pltpu.VMEM((SHARDS, TOTAL + EXTRA, TILE), bf16),
            pltpu.VMEM((SHARDS, 2, TILE, TILE), bf16),
            pltpu.VMEM((TOTAL, SHARDS * TILE), bf16),
            pltpu.VMEM((TOTAL, TILE), f32),
            pltpu.VMEM((TOTAL + ROWS, TILE), bf16),
            pltpu.VMEM((2, ROWS, TILE), bf16),
            pltpu.SemaphoreType.DMA((20,)),
        ],
        compiler_params=limit(56),
        cost_estimate=pl.CostEstimate(
            flops=2 * TOTAL * 2048 * 512, bytes_accessed=6 * 2**20, transcendentals=0
        ),
        name="project_first",
    )(place, gain, *shards, *weights)


def second_kernel(normed_ref, kv_parts, *refs):
    weights, parts = refs[:10], refs[10:12]
    tiles, normed, sent, sems = refs[12:]
    rows = fetch_all([(normed_ref, normed)], sems)
    fetched = block_copies(weights, tiles, 1, 2, sems, 1)
    last = pl.ds(TOTAL, ROWS)
    small = fetch_all([(kv_parts.at[i], sent.at[i, last]) for i in range(2)], sems, 9)
    await_all(rows)
    outgoing = []
    for i in range(2):
        found = product(normed, tiles, i, fetched if i == 0 else None)
        sent[i, pl.ds(0, TOTAL), :] = found.astype(jnp.bfloat16)
        small[i].wait()
        outgoing += fetch_all([(sent.at[i], parts[i])], sems, 11 + i)
    await_all(outgoing)


def project_second(normed, kv_parts, weights):
    bf16 = jnp.bfloat16
    return pl.pallas_call(
        second_kernel,
        out_shape=[shaped((TOTAL + ROWS, TILE), bf16)] * 2,
        in_specs=[ANY] * 12,
        out_specs=[ANY] * 2,
        scratch_shapes=[
            pltpu.VMEM((SHARDS, 2, TILE, TILE), bf16),
            pltpu.VMEM((TOTAL, SHARDS * TILE), bf16),
            pltpu.VMEM((2, TOTAL + ROWS, TILE), bf16),
            pltpu.SemaphoreType.DMA((13,)),
        ],
        compiler_params=limit(56),
        cost_estimate=pl.CostEstimate(
            flops=2 * TOTAL * 2048 * 512, bytes_accessed=6 * 2**20, transcendentals=0
        ),
        name="project_second",
    )(normed, kv_parts, *weights)


def third_kernel(normed_ref, kv_ref, _, *refs):
    weights, own_ref = refs[:10], refs[10]
    tiles, normed, own, sems = refs[11:]
    rows = fetch_all([(normed_ref, normed)], sems)
    fetched = block_copies(weights, tiles, 0, 1, sems, 1)
    small = fetch_all([(kv_ref, own.at[pl.ds(TOTAL, ROWS)])], sems, 9)
    await_all(rows)
    own[pl.ds(0, TOTAL), :] = product(normed, tiles, 0, fetched)
    await_all(small)
    await_all(fetch_all([(own, own_ref)], sems, 10))


def project_third(normed, kv_own, after, weights):
    return pl.pallas_call(
        third_kernel,
        out_shape=shaped((TOTAL + ROWS, TILE), jnp.float32),
        in_specs=[ANY] * 13,
        out_specs=ANY,
        scratch_shapes=[
            pltpu.VMEM((SHARDS, 1, TILE, TILE), jnp.bfloat16),
            pltpu.VMEM((TOTAL, SHARDS * TILE), jnp.bfloat16),
            pltpu.VMEM((TOTAL + ROWS, TILE), jnp.float32),
            pltpu.SemaphoreType.DMA((11,)),
        ],
        compiler_params=limit(56),
        name="project_third",
    )(normed, kv_own, after, *weights)


def gather_kernel(*refs):
    weights, cache_ref, caches, sems = refs[:10], refs[10], refs[11], refs[12]
    outgoing = []
    for p, copy in enumerate(block_copies(weights, caches, 5, 1, sems, 0)):
        copy.wait()
        here = cache_ref.at[pl.ds(p * TILE, TILE)]
        outgoing += fetch_all([(caches.at[p, 0], here)], sems, SHARDS + p)
    await_all(outgoing)


def gather_cache(weights):
    return pl.pallas_call(
        gather_kernel,
        out_shape=shaped((PROMPT_TOKENS, TILE), jnp.bfloat16),
        in_specs=[ANY] * 10,
        out_specs=ANY,
        scratch_shapes=[
            pltpu.VMEM((SHARDS, 1, TILE, TILE), jnp.bfloat16),
            pltpu.SemaphoreType.DMA((2 * SHARDS,)),
        ],
        compiler_params=limit(56),
        name="gather",
    )(*weights)


def rotate(v, cosine, sine):
    return v * cosine + swap_halves(v) * sine


def fresh_kernel(own, p1, p3, cosine, sine, out):
    v = own[...]
    for part in (p1, p3):
        v = v + part[...].astype(jnp.float32)
    out[:, :HEAD_SIZE] = rotate(v[:, :HEAD_SIZE], cosine[...], sine[...]).astype(jnp.bfloat16)
    out[:, HEAD_SIZE:] = v[:, HEAD_SIZE:].astype(jnp.bfloat16)


def fresh_keys(own, parts, cosine, sine):
    last = pl.BlockSpec((ROWS, TILE), lambda i: (OUT_DEV, 0))
    table = pl.BlockSpec((ROWS, HEAD_SIZE), lambda i: (0, 0))
    return pl.pallas_call(
        fresh_kernel,
        out_shape=shaped((ROWS, TILE), jnp.bfloat16),
        grid=(1,),
        in_specs=[last] * 3 + [table] * 2,
        out_specs=pl.BlockSpec((ROWS, TILE), lambda i: (0, 0)),
        compiler_params=limit(4),
        name="fresh",
    )(own, *parts, cosine, sine)


FACTOR = HEAD_SIZE**-0.5 * 1.4426950408889634


def stage_kernel(own_ref, cache_ref, part, own, cache, sems):
    copies = fetch_all([(own_ref, own), (cache_ref, cache)], sems)
    copies[0].wait()
    own[...] += part[...].astype(jnp.float32)
    copies[1].wait()


def stage(own, cache, part):
    return pl.pallas_call(
        stage_kernel,
        out_shape=[shaped(own.shape, own.dtype), shaped(cache.shape, cache.dtype)],
        in_specs=[ANY] * 2 + [VMEM],
        out_specs=[VMEM] * 2,
        scratch_shapes=[pltpu.SemaphoreType.DMA((2,))],
        compiler_params=limit(2),
        name="stage",
    )(own, cache, part)


def prompt_kernel(own, p1, p3, cosine, sine, caches, q_ref, mixed_ref, top_ref, total_ref):
    def step(j, _):
        rows = pl.ds(pl.multiple_of(j * ROWS, ROWS), ROWS)
        q = own[rows, :]
        for part in (p1, p3):
            q = q + part[rows, :].astype(jnp.float32)
        halves = (q[:, :HEAD_SIZE], q[:, HEAD_SIZE:])
        wide_q = jnp.concatenate(
            [rotate(v, cosine[...], sine[...]).astype(jnp.bfloat16) for v in halves], axis=0
        )
        q_ref[j] = wide_q
        scores = [
            lax.dot_general(
                wide_q,
                caches[i * TILE : (i + 1) * TILE, :HEAD_SIZE],
                (((1,), (1,)), ((), ())),
                preferred_element_type=jnp.float32,
            )
            for i in range(8)
        ]
        top = jnp.max(functools.reduce(jnp.maximum, scores), axis=1, keepdims=True)
        scores = [jnp.exp2((v - top) * FACTOR) for v in scores]
        total = jnp.sum(functools.reduce(jnp.add, scores), axis=1, keepdims=True)
        mixed = None
        for i, v in enumerate(scores):
            term = jnp.dot(
                v.astype(jnp.bfloat16),
                caches[i * TILE : (i + 1) * TILE, HEAD_SIZE:],
                preferred_element_type=jnp.float32,
            )
            mixed = term if mixed is None else mixed + term
        mixed_ref[j] = mixed
        top_ref[j] = jnp.broadcast_to(top, (2 * ROWS, HEAD_SIZE))
        total_ref[j] = jnp.broadcast_to(total, (2 * ROWS, HEAD_SIZE))
        return 0

    lax.fori_loop(0, OUT_DEV, step, 0, unroll=2)


def attend_prompt(own, others, cosine, sine, cache):
    per_slot = (OUT_DEV, 2 * ROWS, HEAD_SIZE)
    return pl.pallas_call(
        prompt_kernel,
        out_shape=[shaped(per_slot, jnp.bfloat16)] + [shaped(per_slot, jnp.float32)] * 3,
        in_specs=[VMEM] * 6,
        out_specs=[VMEM] * 4,
        compiler_params=limit(16),
        cost_estimate=pl.CostEstimate(
            flops=4 * 1024 * 2048 * 128, bytes_accessed=2 * 2**20, transcendentals=1024 * 2048
        ),
        name="prompt",
    )(own, *others, cosine, sine, cache)


def finish_kernel(place, slots, q, mixed_ref, top_ref, total_ref, f0, f1, f2, f3, out_ref, fresh):
    y = place[3]
    for r, part in enumerate((f0, f1, f2, f3)):
        fresh[lax.rem(y + YS - r, YS)] = part[...]
    row = lax.broadcasted_iota(jnp.int32, (2 * ROWS, ROWS), 0) % ROWS
    column = lax.broadcasted_iota(jnp.int32, (2 * ROWS, ROWS), 1)
    for j in range(OUT_DEV):
        valid = slots[2 * OUT_DEV + j]
        scores = lax.dot_general(
            q[j],
            fresh[j, :, :HEAD_SIZE],
            (((1,), (1,)), ((), ())),
            preferred_element_type=jnp.float32,
        )
        scores = jnp.where((column <= row) & (column < valid), scores, MASKED_SCORE)
        top = jnp.maximum(top_ref[j], jnp.max(scores, axis=1, keepdims=True))
        scores = jnp.exp2((scores - top) * FACTOR)
        rescale = jnp.exp2((top_ref[j] - top) * FACTOR)
        total = total_ref[j] * rescale + jnp.sum(scores, axis=1, keepdims=True)
        mixed = mixed_ref[j] * rescale + jnp.dot(
            scores.astype(jnp.bfloat16),
            fresh[j, :, HEAD_SIZE:],
            preferred_element_type=jnp.float32,
        )
        mixed = jnp.where(row < valid, mixed / total, 0.0).astype(jnp.bfloat16)
        out_ref[j, :, :HEAD_SIZE] = mixed[:ROWS]
        out_ref[j, :, HEAD_SIZE:] = mixed[ROWS:]


def finish(place, slots, prompt, fresh):
    return pl.pallas_call(
        finish_kernel,
        out_shape=shaped((OUT_DEV, ROWS, TILE), jnp.bfloat16),
        in_specs=[SMEM] * 2 + [VMEM] * 8,
        out_specs=VMEM,
        scratch_shapes=[pltpu.VMEM((OUT_DEV, ROWS, TILE), jnp.bfloat16)],
        compiler_params=limit(8),
        name="finish",
    )(place, slots, *prompt, *fresh)


def body(
    hidden,
    norm_gain,
    w_query,
    key_projection_weight,
    value_projection_weight,
    prompt_key_cache,
    prompt_value_cache,
    keep_flag,
    destination,
    row_counts,
):
    g = lax.axis_index("group")
    f = lax.axis_index("fsdp")
    place = jnp.stack([g // CORES, g % CORES, f // YS, f % YS]).astype(jnp.int32)
    tie = lax.optimization_barrier

    *pieces, part1, part2, part3, own_parts = pack(
        keep_flag,
        destination,
        hidden,
        w_query,
        key_projection_weight,
        value_projection_weight,
        prompt_key_cache,
        prompt_value_cache,
    )

    for r in (1, 3, 2):
        pieces[r] = send_x(pieces[r], r)
    pieces[0], pieces[1] = tie((pieces[0], pieces[1]))
    slots, pieces[0] = plan(place, keep_flag, destination, row_counts, pieces[0])
    arrived = [send_y(part1, -1), send_y(part2, -2), send_y(part3, -3)]
    pieces, arrived[0] = tie((pieces, arrived[0]))
    inward, outward = sort_pieces(slots, pieces)
    rows, sums = unpack(slots, inward, swap(outward))
    sums = [sums] + [send_y(sums, r) for r in (1, 2, 3)]

    sums, arrived = tie((sums, arrived))
    rows = label(rows, sums)
    arrived = jnp.stack([arrived[0], arrived[2], arrived[1]])
    own = jnp.concatenate([own_parts[:1], arrived, own_parts[1:]], axis=0)
    near, next_ = send_x(own, 1), send_x(own, -1)
    rows, own = tie((rows, own))
    a1, b1, own_swapped = send_z(rows, 1), send_z(rows, -1), swap(own)
    a1, b1, own_swapped = tie((a1, b1, own_swapped))
    a2, b2 = send_z(b1, 1), send_z(a1, -1)
    a2, b2, near, next_ = tie((a2, b2, near, next_))
    a3, b3 = send_z(b2, 1), send_z(a2, -1)
    far_a, far_b = send_x(next_[:3], 1), send_x(near[3:], -1)
    a3, b3, far_a, far_b, near, next_ = tie((a3, b3, far_a, far_b, near, next_))
    far, near_swapped, next_swapped = send_z(b3, 1), swap(near), swap(next_)
    far_a_swapped, far_b_swapped = swap(far_a), swap(far_b)
    shards = [rows, a1, a2, a3, b1, b2, b3, far]
    weights = [own, near, next_, far_a, far_b]
    weights += [own_swapped, near_swapped, next_swapped, far_a_swapped, far_b_swapped]
    gain = norm_gain.astype(jnp.float32).reshape(ZS * YS, TILE)
    cache = gather_cache(weights)
    gain, cache = tie((gain, cache))
    normed, part2, kv_own, kv_parts = project_first(place, gain, shards, weights)
    part2 = send_y(part2, 2)
    part1, part3 = project_second(normed, kv_parts, weights)

    parts = [send_y(part1, 1), send_y(part3, 3)]
    q_own = project_third(normed, kv_own, part1, weights)
    q_own, cache = stage(q_own, cache, part2)
    cosine, sine = rope_tables(ROWS, PROMPT_TOKENS)
    fresh = fresh_keys(q_own, parts, cosine, sine)
    fresh = [fresh] + [send_y(fresh, r) for r in (1, 2, 3)]
    prompt = attend_prompt(q_own, parts, cosine, sine, cache)
    return finish(place, slots, prompt, fresh)


def solution(mesh):
    return jax.shard_map(
        body,
        mesh=mesh,
        in_specs=(
            P("group", None, "fsdp"),
            P(),
            P("group", "fsdp"),
            P("group", None),
            P("group", None),
            P("group", None),
            P("group", None),
            P(),
            P(),
            P(),
        ),
        out_specs=P("group", None, "fsdp"),
        check_vma=False,
    )
```
